32 devices in a mesh: expert: 8 (over z, y), tensor: 4 (over x, core).
Axes of the slice: x: 2, y: 2, z: 4, core: 2. Of those that a mesh axis runs over, the one named last changes fastest.
Arguments:
- tokens: bfloat16 [2048, 2048], P('expert'), may hold values from -6 to 6
- cotangent: bfloat16 [2048, 2048], P('expert'), may hold values from -8 to 8
- segment_ids: int32 [8, 256], P('expert'), may hold values from 0 to 3, never falling along the last dimension, each value on 1 to 128 neighbouring positions
- routes_att: int32 [2048, 2], P('expert'), may hold values from 0 to 7, all different within a row; in each aligned block of 256 rows (0 to 255, 256 to 511, ...) at most 96 rows name the same one
- routes_mlp: int32 [2048, 2], P('expert'), may hold values from 0 to 7, all different within a row; in each aligned block of 256 rows (0 to 255, 256 to 511, ...) at most 96 rows name the same one
- gain_att: bfloat16 [2048], P('expert'), may hold values from 0.5 to 1.5
- router_att: bfloat16 [2048, 8], P('expert'), may hold values from -0.125 to 0.125
- w_query: bfloat16 [2048, 8, 2048], P('expert', None, 'tensor'), may hold values from -0.125 to 0.125
- w_key: bfloat16 [2048, 2048], P('expert', 'tensor'), may hold values from -0.125 to 0.125
- w_value: bfloat16 [2048, 2048], P('expert', 'tensor'), may hold values from -0.125 to 0.125
- w_output: bfloat16 [2048, 8, 2048], P('expert', None, 'tensor'), may hold values from -1 to 1
- gain_mlp: bfloat16 [2048], P('expert'), may hold values from 0.5 to 1.5
- router_mlp: bfloat16 [2048, 8], P('expert'), may hold values from -0.125 to 0.125
- w_gate: bfloat16 [8, 2048, 5632], P('expert', None, 'tensor'), may hold values from -0.125 to 0.125
- w_up: bfloat16 [8, 2048, 5632], P('expert', None, 'tensor'), may hold values from -0.125 to 0.125
- w_down: bfloat16 [8, 5632, 2048], P('expert', 'tensor'), may hold values from -0.078125 to 0.078125
Outputs:
- mixed_out: bfloat16 [2048, 2048], P('expert')
- grad_tokens: float32 [2048, 2048], P('expert')
- grad_gain_att: float32 [2048], P('expert')
- grad_router_att: float32 [2048, 8], P('expert')
- grad_query: float32 [2048, 8, 2048], P('expert', None, 'tensor')
- grad_key: float32 [2048, 2048], P('expert', 'tensor')
- grad_value: float32 [2048, 2048], P('expert', 'tensor')
- grad_output: float32 [2048, 8, 2048], P('expert', None, 'tensor')
- grad_gain_mlp: float32 [2048], P('expert')
- grad_router_mlp: float32 [2048, 8], P('expert')
- grad_gate: float32 [8, 2048, 5632], P('expert', None, 'tensor')
- grad_up: float32 [8, 2048, 5632], P('expert', None, 'tensor')
- grad_down: float32 [8, 5632, 2048], P('expert', 'tensor')
The draws below stay inside these ranges and needn't reach their ends.
Inputs may be any that keep to these rules, and one draw needn't show every extreme that they name: `segment_ids`: document numbers never fall along a sequence; each document has 1 to 128 positions, one exactly that many. `routes_att`: each row names two different attention experts; in the rows of one sequence no expert is named more than 96 times, and in some sequence one expert exactly 96 times. `routes_mlp`: each row names two different feed-forward experts; in the rows of one sequence no expert is named more than 96 times, and in some sequence one expert exactly 96 times.
All inputs are finite; a program needn't handle non-finite values.
Results may differ from the reference program's by a relative error of at most 0.014.
Values may be sent and summed in bfloat16 or wider, within the bound.
No kernel may reach another device: no remote copies, remote signals or barrier semaphores. Data moves between devices by JAX's collectives and lax.ppermute only.
A program may use at most 320 MiB of HBM per device.

```python
import math
import jax
import jax.numpy as jnp
import numpy as np
from jax import lax

D = 2048
HEADS = 16
HEAD_DIM = 128
EA = 8
EXPERTS = 8
FF = 5632
TOK_DEV = 256
CAP = 96
GROUP = 1
SEQS = 8
TOKENS = 2048
N_EXPERT = 8
N_TENSOR = 4


def spiked(values, stream_key, source, target, parts, factor):
    def block_of(axis_at):
        return (jnp.arange(values.shape[axis_at]) // (values.shape[axis_at] // parts)).reshape((-1,) + (1,) * (values.ndim - 1 - axis_at))

    one_side = jax.random.permutation(stream_key, parts)[block_of(target)]
    second = (block_of(target) + parts // 2) % parts
    return jnp.where((block_of(source) == one_side) | (block_of(source) == second), factor * values, values)


def level_of(own_key, dims, cuts, least, top_value):
    loudness = 1.0
    for position, parts in cuts:
        draws = jax.random.uniform(jax.random.fold_in(jax.random.fold_in(own_key, 6), position), (parts,), jnp.float32, least / len(cuts), top_value / len(cuts))
        loudness = loudness * jnp.repeat(jnp.exp(draws), dims[position] // parts).reshape((-1,) + (1,) * (len(dims) - 1 - position))
    return loudness


def profile(count, total, most, slope):
    loads = [(1 << 20) // math.isqrt(grade ** slope) + 1 for grade in range(2, count + 1)]
    surplus, holding = total - most - (count - 1), [1] * (count - 1)
    while surplus > 0:
        candidates = [i for i in range(count - 1) if holding[i] < most]
        mass, budget = sum([loads[i] for i in candidates]), surplus
        for i in candidates:
            more = min(most - holding[i], max(1, budget * loads[i] // mass), surplus)
            holding[i] = holding[i] + more
            surplus = surplus - more
    return np.array([most] + holding)


def uneven_parts(stream_key, count, total, most, skew):
    if count == 2:
        one = jax.random.randint(stream_key, (), max(1, total - most), min(most, total - 1) + 1)
        return jnp.stack([one, total - one])
    tallies = jnp.asarray(profile(count, total, most, skew), jnp.int32)
    couples = (count - 1) // 2
    source_of, receiver = tallies[1:1 + 2 * couples:2], tallies[2:2 + 2 * couples:2]
    room = jnp.minimum(source_of - 1, most - receiver)
    passed = jax.random.randint(jax.random.fold_in(stream_key, 1), (couples,), 0, 1 << 20) % (room + 1)
    tallies = tallies.at[1:1 + 2 * couples:2].set(source_of - passed).at[2:2 + 2 * couples:2].set(receiver + passed)
    return tallies[jax.random.permutation(jax.random.fold_in(stream_key, 2), count)]


def assign_block(key, own, number, rows, count, top, limit, slope):
    order = jax.random.permutation(key, count)
    heavy_load, ordinary = load_shares(count, rows * top, limit, slope, True), load_shares(count, rows * top, limit, slope, False)
    places = jnp.arange(count)

    def named(sizes, offset_by):
        used = int((sizes > 0).sum())
        fixed = max(1, used // 4)
        shifted = fixed + (places - fixed + offset_by * (used - fixed)) % max(1, count - fixed)
        return jnp.zeros((count,), jnp.int32).at[order[jnp.where(places < fixed, places, shifted)]].set(jnp.asarray(sizes, jnp.int32))

    sizes = jnp.where(number % 4 == 0, named(heavy_load, number // 4), named(ordinary, number - number // 4 - 1))
    mixed = jax.random.permutation(jax.random.fold_in(own, 3), count)
    giver, receiver = mixed[0:count // 2 * 2:2], mixed[1:count // 2 * 2:2]
    slack = jnp.minimum(sizes[giver] - 1, limit - sizes[receiver]) // 2
    slack = jnp.where((giver == order[0]) | (receiver == order[0]) | (sizes[receiver] == 0), 0, jnp.maximum(slack, 0))
    shifted = jax.random.randint(jax.random.fold_in(own, 4), (count // 2,), 0, 1 << 20) % (slack + 1)
    sizes = sizes.at[giver].add(-shifted).at[receiver].add(shifted)
    items = jnp.searchsorted(jnp.cumsum(sizes), jnp.arange(rows * top), side="right").astype(jnp.int32)
    grid = items.reshape(top, rows).T
    grid = grid[jax.random.permutation(jax.random.fold_in(own, 1), rows)]
    offset_by = jax.random.randint(jax.random.fold_in(own, 2), (rows, 1), 0, top)
    return jnp.take_along_axis(grid, (jnp.arange(top)[None, :] + offset_by) % top, axis=1)


def load_shares(count, total, limit, slope, full):
    loads = [(1 << 20) // math.isqrt(grade ** slope) + 1 for grade in range(1, count + 1)]
    largest = limit if full else min(limit, max(-(-total // count), total * loads[0] // sum(loads)))
    least = 1 if total - largest >= count - 1 else 0
    given, surplus = [largest] + [least] * (count - 1), total - largest - least * (count - 1)
    while surplus > 0:
        candidates = [i for i in range(1, count) if given[i] < largest] or [i for i in range(1, count) if given[i] < limit]
        whole, left = sum([loads[i] for i in candidates]), surplus
        for i in candidates:
            extra = min(limit - given[i], max(1, left * loads[i] // whole), surplus)
            given[i] = given[i] + extra
            surplus = surplus - extra
    return np.array(given)


def centred(own_key, extent, scale, most, shards=(), kind=jnp.bfloat16):
    factor_of = level_of(own_key, extent, shards, -0.22, 0.18) if shards else 1.0
    values = jax.random.normal(own_key, extent, jnp.float32) * scale * factor_of
    return jnp.minimum(jnp.maximum(values, -most), most).astype(kind)


def noise_with(rng, dims, scale, most, cuts, heavy, held_as=jnp.bfloat16):
    drawn = scale * jax.random.normal(rng, dims, jnp.float32)
    if cuts:
        drawn = drawn * level_of(rng, dims, cuts, -0.22, 0.18)
    return jnp.clip(spiked(drawn, jax.random.fold_in(rng, 3), *heavy), -most, most).astype(held_as)


def setup_inputs(seed: int = 0) -> dict:
    arg_keys = jax.random.split(jax.random.key(seed), 17)
    tokens = centred(arg_keys[0], (TOKENS, D), 1.0, 6.0, ((0, 8),))
    cotangent = noise_with(arg_keys[1], (TOKENS, D), 1.0, 8.0, ((0, 8),), (0, 1, 8, 2.0))
    segment_ids = jax.vmap(lambda own: jnp.searchsorted(jnp.cumsum(uneven_parts(own, 4, TOK_DEV, TOK_DEV // 2, 2)), jnp.arange(TOK_DEV), side="right"))(jax.random.split(arg_keys[2], SEQS)).reshape((SEQS, TOK_DEV)).astype(jnp.int32)
    routes_att_keys = jax.random.split(jax.random.fold_in(arg_keys[3], 1), TOKENS // TOK_DEV)
    routes_att_turns = jax.random.permutation(jax.random.fold_in(arg_keys[3], 3), TOKENS // TOK_DEV)
    routes_att = jax.vmap(lambda own, number: assign_block(jax.random.fold_in(arg_keys[3], 2), own, number, TOK_DEV, EA, 2, CAP, 1))(routes_att_keys, routes_att_turns).reshape((TOKENS, 2))
    routes_mlp_keys = jax.random.split(jax.random.fold_in(arg_keys[4], 1), TOKENS // TOK_DEV)
    routes_mlp_turns = jax.random.permutation(jax.random.fold_in(arg_keys[4], 3), TOKENS // TOK_DEV)
    routes_mlp = jax.vmap(lambda own, number: assign_block(jax.random.fold_in(arg_keys[4], 2), own, number, TOK_DEV, EXPERTS, 2, CAP, 1))(routes_mlp_keys, routes_mlp_turns).reshape((TOKENS, 2))
    gain_att = jnp.clip(1.0 + 0.1 * jax.random.normal(arg_keys[5], (D,), jnp.float32), 0.5, 1.5).astype(jnp.bfloat16)
    router_att = centred(arg_keys[6], (D, EA), D ** -0.5, 0.125, ((0, 8),))
    w_query = centred(arg_keys[7], (D, EA, HEADS * HEAD_DIM), D ** -0.5, 0.125, ((0, 8), (2, 4)))
    w_key = centred(arg_keys[8], (D, HEADS * HEAD_DIM), D ** -0.5, 0.125, ((0, 8), (1, 4)))
    w_value = centred(arg_keys[9], (D, HEADS * HEAD_DIM), D ** -0.5, 0.125, ((0, 8), (1, 4)))
    w_output = centred(arg_keys[10], (D, EA, HEADS * HEAD_DIM), (max(HEADS * HEAD_DIM // 64, 1)) ** -0.5, 1.0, ((0, 8), (2, 4)))
    gain_mlp = jnp.clip(1.0 + 0.1 * jax.random.normal(arg_keys[11], (D,), jnp.float32), 0.5, 1.5).astype(jnp.bfloat16)
    router_mlp = centred(arg_keys[12], (D, EXPERTS), D ** -0.5, 0.125, ((0, 8),))
    w_gate = centred(arg_keys[13], (N_EXPERT, D, FF // GROUP), D ** -0.5, 0.125, ((0, 8), (2, 4)))
    w_up = centred(arg_keys[14], (N_EXPERT, D, FF // GROUP), D ** -0.5, 0.125, ((0, 8), (2, 4)))
    w_down = centred(arg_keys[15], (N_EXPERT, FF // GROUP, D), FF ** -0.5, 0.078125, ((0, 8), (1, 4)))
    return dict(tokens=tokens, cotangent=cotangent, segment_ids=segment_ids, routes_att=routes_att, routes_mlp=routes_mlp, gain_att=gain_att, router_att=router_att, w_query=w_query, w_key=w_key, w_value=w_value, w_output=w_output, gain_mlp=gain_mlp, router_mlp=router_mlp, w_gate=w_gate, w_up=w_up, w_down=w_down)


@jax.custom_vjp
def low(v):
    return lax.optimization_barrier(v.astype(jnp.bfloat16)).astype(jnp.float32)

@jax.custom_vjp
def low_back(v):
    return v

def low_keep(v):
    return (low(v), None)

def low_pass(kept, grad):
    return (grad,)

def back_keep(v):
    return (v, None)

def back_low(kept, grad):
    return (low(grad),)
low.defvjp(low_keep, low_pass)
low_back.defvjp(back_keep, back_low)
EPSILON = 1e-05
ROTARY_BASE = 10000.0
PRECISE = lax.Precision.HIGHEST

def slot_table(route_pairs, count_kinds, capacity, part_count):
    flat_kind = route_pairs.reshape(-1).astype(jnp.int32)
    total_rows = flat_kind.shape[0]
    onehot = (flat_kind[:, None] == jnp.arange(count_kinds, dtype=jnp.int32)[None, :]).astype(jnp.int32)
    ranking = lax.optimization_barrier(jnp.sum((jnp.cumsum(onehot, axis=0) - 1) * onehot, axis=1)).astype(jnp.int32)
    quarter = capacity // part_count
    slot_of = ranking // quarter * (count_kinds * quarter) + flat_kind * quarter + ranking % quarter
    slot_of = slot_of.astype(jnp.int32)
    source_rows = jnp.zeros((count_kinds * capacity,), jnp.int32).at[slot_of].set(jnp.arange(total_rows, dtype=jnp.int32))
    filled = jnp.zeros((count_kinds * capacity,), jnp.int32).at[slot_of].set(1)
    return (source_rows, filled, slot_of.reshape(route_pairs.shape))

def angles(length, width, dtype):
    half_width = width // 2
    freqs = ROTARY_BASE ** (-(jnp.arange(half_width, dtype=dtype) * 2.0 / width))
    phase = jnp.arange(length, dtype=dtype)[:, None] * freqs[None, :]
    phase = jnp.concatenate([phase, phase], axis=1)
    return (jnp.cos(phase), jnp.sin(phase))

def rotate(values, cosine, sine_table):
    half_width = values.shape[-1] // 2
    turned = jnp.concatenate([-values[..., half_width:], values[..., :half_width]], axis=-1)
    return values * cosine + turned * sine_table

def root_norm(values, gain):
    factor = lax.rsqrt(lax.optimization_barrier(jnp.mean(values * values, axis=-1, keepdims=True)) + EPSILON)
    return values * factor * gain

def pair_gates(logits, route_pairs):
    chosen = jnp.take_along_axis(logits, route_pairs, axis=-1)
    return jax.nn.softmax(chosen, axis=-1)

def attend(weights, pieces):
    gain_att, router_att, w_query, w_key, w_value, w_output = weights
    block_rows, segment, route_pairs = pieces
    length = block_rows.shape[0]
    normed = low(root_norm(block_rows, gain_att))
    gate_pair = pair_gates(jnp.dot(normed, router_att, precision=PRECISE), route_pairs)
    source_rows, filled, slot_of = slot_table(route_pairs, EA, CAP, 1)
    keep_rows = filled[:, None].astype(normed.dtype)
    row_buf = (normed[source_rows // 2] * keep_rows).reshape(EA, CAP, D)
    query_buf = jnp.einsum('ecd,deh->ech', row_buf, w_query, precision=PRECISE).reshape(EA * CAP, HEADS * HEAD_DIM)
    query_raw = query_buf[slot_of].reshape(length, 2, HEADS, HEAD_DIM)
    cosine, sine_table = angles(length, HEAD_DIM, block_rows.dtype)
    query = low(rotate(low_back(query_raw), cosine[:, None, None, :], sine_table[:, None, None, :]))
    key_raw = jnp.dot(normed, w_key, precision=PRECISE).reshape(length, HEADS, HEAD_DIM)
    key_rot = low(rotate(low_back(key_raw), cosine[:, None, :], sine_table[:, None, :]))
    value_heads = low(low_back(jnp.dot(normed, w_value, precision=PRECISE))).reshape(length, HEADS, HEAD_DIM)
    scores = low_back(jnp.einsum('tchd,uhd->chtu', query, key_rot, precision=PRECISE) * HEAD_DIM ** (-0.5))
    places = jnp.arange(length)
    allowed = (segment[:, None] == segment[None, :]) & (places[None, :] <= places[:, None])
    scores = jnp.where(allowed, scores, -1e+30)
    weights_low = low(jax.nn.softmax(scores, axis=-1))
    mixed_heads = low(low_back(jnp.einsum('chtu,uhd->tchd', weights_low, value_heads, precision=PRECISE)))
    mixed_heads = mixed_heads.reshape(2 * length, HEADS * HEAD_DIM)
    out_rows = (mixed_heads[source_rows] * keep_rows).reshape(EA, CAP, HEADS * HEAD_DIM)
    branch_buf = jnp.einsum('ech,deh->ecd', out_rows, w_output, precision=PRECISE).reshape(EA * CAP, D)
    branch = low_back(branch_buf[slot_of])
    return block_rows + lax.optimization_barrier(jnp.sum(gate_pair[:, :, None] * branch, axis=1))

def expert(row_buf, gate_full, up_full, down_full):
    gate_pre = low_back(jnp.dot(row_buf, gate_full, precision=PRECISE))
    up_pre = low_back(jnp.dot(row_buf, up_full, precision=PRECISE))
    acted = low(jax.nn.silu(gate_pre) * up_pre)
    return low_back(low(jnp.dot(acted, down_full, precision=PRECISE)))

def make_forward(segment_ids, routes_att, routes_mlp):

    def forward(tokens, gain_att, router_att, w_query, w_key, w_value, w_output, gain_mlp, router_mlp, w_gate, w_up, w_down):
        blocks = tokens.reshape(SEQS, TOK_DEV, D)
        att_pairs = routes_att.reshape(SEQS, TOK_DEV, 2)
        mlp_pairs = routes_mlp.reshape(SEQS, TOK_DEV, 2)
        weights = (gain_att, router_att, w_query, w_key, w_value, w_output)
        checked_attend = jax.checkpoint(attend)

        def attend_one(pieces):
            return checked_attend(weights, pieces)
        hidden = lax.map(attend_one, (blocks, segment_ids, att_pairs))
        normed_two = low(root_norm(hidden, gain_mlp))
        gates_two = pair_gates(jnp.einsum('btd,de->bte', normed_two, router_mlp, precision=PRECISE), mlp_pairs)

        def table_one(route_pairs):
            return slot_table(route_pairs, EXPERTS, CAP, N_TENSOR)
        source_rows, filled, slot_of = jax.vmap(table_one)(mlp_pairs)

        def fill_rows(normed, source, kept):
            return normed[source // 2] * kept[:, None].astype(normed.dtype)
        quarter = CAP // N_TENSOR
        row_buf = jax.vmap(fill_rows)(normed_two, source_rows, filled)
        row_buf = row_buf.reshape(SEQS, N_TENSOR, EXPERTS, quarter, D).transpose(2, 0, 1, 3, 4).reshape(EXPERTS, SEQS * CAP, D)
        group_size = N_EXPERT // EXPERTS
        part_width = FF // group_size
        gate_full = w_gate.reshape(EXPERTS, group_size, D, part_width).transpose(0, 2, 1, 3).reshape(EXPERTS, D, FF)
        up_full = w_up.reshape(EXPERTS, group_size, D, part_width).transpose(0, 2, 1, 3).reshape(EXPERTS, D, FF)
        down_full = w_down.reshape(EXPERTS, FF, D)
        checked_expert = jax.checkpoint(expert)

        def expert_one(pieces):
            return checked_expert(pieces[0], pieces[1], pieces[2], pieces[3])
        outputs = lax.map(expert_one, (row_buf, gate_full, up_full, down_full))
        outputs = outputs.reshape(EXPERTS, SEQS, N_TENSOR, quarter, D).transpose(1, 2, 0, 3, 4).reshape(SEQS, EXPERTS * CAP, D)

        def pick_rows(output_rows, slots_here):
            return output_rows[slots_here]
        expert_out = jax.vmap(pick_rows)(outputs, slot_of)
        final = hidden + lax.optimization_barrier(jnp.sum(gates_two[..., None] * expert_out, axis=2))
        return final.reshape(TOKENS, D)
    return forward

def reference(tokens, cotangent, segment_ids, routes_att, routes_mlp, gain_att, router_att, w_query, w_key, w_value, w_output, gain_mlp, router_mlp, w_gate, w_up, w_down):
    forward = make_forward(segment_ids, routes_att, routes_mlp)
    inputs = (tokens, gain_att, router_att, w_query, w_key, w_value, w_output, gain_mlp, router_mlp, w_gate, w_up, w_down)
    floats = tuple((array.astype(jnp.float32) for array in inputs))
    result, pullback = jax.vjp(forward, *floats)
    grads = pullback(cotangent.astype(jnp.float32))
    return (result.astype(jnp.bfloat16), grads[0], grads[1], grads[2], grads[3], grads[4], grads[5], grads[6], grads[7], grads[8], grads[9], grads[10], grads[11])
```

```python
import functools

import jax
import jax.numpy as jnp
from jax import lax
from jax.experimental import pallas as pl
from jax.experimental.pallas import tpu as pltpu
from jax.sharding import PartitionSpec as P

D = 2048
HEAD_DIM = 128
EA = 8
EXPERTS = 8
CAP = 96
EPSILON = 1e-05
ROTARY_BASE = 10000.0
VMEM = 56 * 1024 * 1024
F32 = jnp.float32
BF16 = jnp.bfloat16
PRECISE = lax.Precision.HIGHEST


def hop(values, axis, bit):
    size = lax.axis_size(axis)
    return lax.ppermute(values, axis, [(i, i ^ bit) for i in range(size)])


def bits_of(axis):
    size, bits = lax.axis_size(axis), []
    while 1 << len(bits) < size:
        bits.append(1 << len(bits))
    return bits[::-1]


def gather_pieces(values, axis, bits=None):
    pieces = {0: values}
    for bit in bits_of(axis) if bits is None else bits:
        for known in sorted(pieces):
            pieces[known | bit] = hop(pieces[known], axis, bit)
    return pieces


def scatter_sum(chunks, axis, bits=None, sent_as=None):
    held, came = dict(chunks), []
    for bit in (bits_of(axis) if bits is None else bits)[::-1]:
        for k in sorted(held, reverse=True):
            if k & bit:
                sent = held.pop(k)
                came.append(hop(sent.astype(sent_as or sent.dtype), axis, bit))
                held[k ^ bit] = held[k ^ bit].astype(F32) + came[-1].astype(F32)
                if k ^ bit:
                    held[k ^ bit] = held[k ^ bit].astype(sent_as or sent.dtype)
    return held[0], came


def after(values, *earlier):
    return lax.optimization_barrier((values, *earlier))[0]


def whole_spec(shape):
    zeros = (0,) * len(shape)
    return pl.BlockSpec(shape, lambda *_: zeros)


def params(*arrays):
    held = 3 * sum(one.size * one.dtype.itemsize for one in arrays) + (12 << 20)
    return pltpu.CompilerParams(vmem_limit_bytes=min(VMEM, held) if arrays else 16 << 20)


def one_of(routes, kind):
    return (routes == kind).astype(F32).astype(BF16)


def map_of(refs, kind):
    each = EA // len(refs)
    return refs[kind // each][kind % each]


def project_kernel(which, counts, *refs):
    x_refs, refs = refs[: len(counts)], refs[len(counts) :]
    w_refs = []
    for count in counts:
        w_refs.append(refs[:count])
        refs = refs[count:]
    routes_ref, outs = refs[0], refs[1:]
    for at, k in enumerate(which):
        routes = routes_ref[k // 2]
        for choice in range(2):
            total = jnp.zeros(outs[0].shape, F32)
            for x_ref, maps in zip(x_refs, w_refs):
                x = x_ref[k // 2]
                each = EA // len(maps)
                for first, w_ref in zip(range(0, EA, each), maps):
                    spread = jnp.concatenate(
                        [
                            x * one_of(routes[:, choice : choice + 1], kind)
                            for kind in range(first, first + each)
                        ],
                        axis=1,
                    )
                    flat = w_ref[...].reshape(each * x.shape[1], w_ref.shape[2])
                    total += jnp.dot(spread, flat, preferred_element_type=F32)
            outs[2 * at + choice][...] = total.astype(outs[0].dtype)


def project(which, xs, ws, routes, dtype):
    _, length, depth = xs[0].shape
    width = ws[0][0].shape[2]
    outs = [jax.ShapeDtypeStruct((length, width), dtype)] * (2 * len(which))
    maps = [one for side in ws for one in side]
    return pl.pallas_call(
        functools.partial(project_kernel, which, [len(side) for side in ws]),
        out_shape=outs,
        compiler_params=params(*xs, *maps, *outs),
    )(*xs, *maps, routes)


def contract_kernel(which, counts, parts, routes_ref, *refs):
    w_refs = []
    for count in counts:
        w_refs.append(refs[:count])
        refs = refs[count:]
    rows, outs = refs[: 2 * len(which)], refs[2 * len(which) :]
    share, depth = outs[0].shape[1], w_refs[0][0].shape[1]
    turned = (((1,), (1,)), ((), ()))
    for at, k in enumerate(which):
        routes = routes_ref[k // 2]
        first, second = rows[2 * at][...], rows[2 * at + 1][...]
        totals = [jnp.zeros((share * parts, depth), F32)] * len(counts)
        for kind in range(EA):
            ones = one_of(routes, kind)
            picked = first * ones[:, 0:1] + second * ones[:, 1:2]
            totals = [
                total
                + lax.dot_general(picked, map_of(maps, kind), turned, preferred_element_type=F32)
                for total, maps in zip(totals, w_refs)
            ]
        for b, total in enumerate(totals):
            for r in range(parts):
                outs[r][at, :, b * depth : (b + 1) * depth] = total[
                    r * share : (r + 1) * share
                ].astype(outs[r].dtype)


def contract(which, pieces, routes, ws, parts):
    rows = [half for k in which for half in pieces[k]]
    _, length, _ = routes.shape
    depth, width = ws[0][0].shape[1:]
    shape = (len(which), length // parts, depth * len(ws))
    maps = [one for side in ws for one in side]
    return pl.pallas_call(
        functools.partial(contract_kernel, which, [len(side) for side in ws], parts),
        out_shape=[
            jax.ShapeDtypeStruct(shape, BF16 if r % 2 else F32) for r in range(parts)
        ],
        compiler_params=params(*maps, *rows),
    )(routes, *maps, *rows)


def to_owners(pieces, routes, ws, parts, ties=((), ())):
    came, order = {}, sorted(pieces)
    for which, tie in zip((order[:-1], order[-1:]), ties):
        chunks = dict(enumerate(contract(tuple(which), pieces, after(routes, *tie), ws, parts)))
        summed, _ = scatter_sum(chunks, "tensor", None, BF16)
        for at, k in enumerate(which):
            came[k] = hop(summed[at].astype(BF16), "expert", k) if k else summed[at]
    return came


def arrange_kernel(parts, places, x_ref, out_ref):
    count, length, depth = out_ref.shape
    share = length // parts
    for r in range(parts):
        spot = pl.ds(pl.multiple_of((places[1] ^ r) * share, share), share)
        for j in range(count):
            out_ref[places[0] ^ j, r * share : (r + 1) * share, :] = x_ref[
                spot, j * depth : (j + 1) * depth
            ]


def arrange(places, x, parts, count):
    shape = (count, x.shape[0], x.shape[1] // count)
    return pl.pallas_call(
        functools.partial(arrange_kernel, parts),
        out_shape=jax.ShapeDtypeStruct(shape, BF16),
        grid_spec=pltpu.PrefetchScalarGridSpec(
            num_scalar_prefetch=1,
            grid=(1,),
            in_specs=[whole_spec(x.shape)],
            out_specs=whole_spec(shape),
        ),
        compiler_params=params(x),
    )(places, x)


def pack_kernel(parts, places, x_ref, routes_ref, blocks_ref, scale_ref, *outs):
    count, length, depth = blocks_ref.shape
    share = length // parts
    for r in range(parts):
        spot = pl.ds(pl.multiple_of((places[1] ^ r) * share, share), share)
        rows = slice(r * share, (r + 1) * share)
        squares = jnp.zeros((share, 1), F32)
        for j in range(count):
            block = x_ref[spot, j * depth : (j + 1) * depth]
            blocks_ref[places[0] ^ j, rows, :] = block
            wide = block.astype(F32)
            squares += jnp.sum(wide * wide, axis=1, keepdims=True)
        scale = lax.rsqrt(squares / D + EPSILON)
        scale_ref[rows, :] = scale
        if r == 0:
            high = scale.astype(BF16).astype(F32)
            middle = (scale - high).astype(BF16).astype(F32)
            routes = routes_ref[spot, :].astype(F32)
            columns = [routes[:, 0:1], routes[:, 1:2], high, middle, scale - high - middle]
            lane = lax.broadcasted_iota(jnp.int32, (share, 128), 1)
            extra = jnp.zeros((share, 128), F32)
            for at, column in enumerate(columns):
                extra = jnp.where(lane == at, column, extra)
    for at, out_ref in enumerate(outs):
        for b in range(2):
            out_ref[:, b * depth : (b + 1) * depth] = blocks_ref[2 * at + b, :share, :]
        out_ref[:, 2 * depth :] = extra.astype(BF16)


def pack(places, x, routes, parts, count):
    length, depth = x.shape[0], x.shape[1] // count
    shapes = [(count, length, depth), (length, 1)]
    shapes += [(length // parts, 2 * depth + 128)] * (count // 2)
    types = [BF16, F32] + [BF16] * (count // 2)
    blocks, scale, *chunks = pl.pallas_call(
        functools.partial(pack_kernel, parts),
        out_shape=[jax.ShapeDtypeStruct(*one) for one in zip(shapes, types)],
        grid_spec=pltpu.PrefetchScalarGridSpec(
            num_scalar_prefetch=1,
            grid=(1,),
            in_specs=[whole_spec(x.shape), whole_spec(routes.shape)],
            out_specs=[whole_spec(one) for one in shapes],
        ),
        compiler_params=params(x),
    )(places, x, routes)
    return blocks, scale, chunks


def unpack_kernel(parts, *refs):
    pieces, (gain_ref, *outs, routes_ref) = refs[:parts], refs[parts:]
    share, depth = pieces[0].shape[1], outs[0].shape[2]
    for r, piece in enumerate(pieces):
        rows = slice(r * share, (r + 1) * share)
        for k in range(piece.shape[0]):
            extra = piece[k, :, 2 * depth :].astype(F32)
            scale = extra[:, 2:3] + extra[:, 3:4] + extra[:, 4:5]
            routes_ref[k, rows, :] = extra[:, 0:2].astype(jnp.int32)
            for b, out_ref in enumerate(outs):
                values = piece[k, :, b * depth : (b + 1) * depth].astype(F32)
                out_ref[k, rows, :] = (values * scale * gain_ref[b : b + 1, :]).astype(BF16)


def unpack(pieces, gains):
    count, share, _ = pieces[0].shape
    shape = (count, share * len(pieces), gains.shape[1])
    return pl.pallas_call(
        functools.partial(unpack_kernel, len(pieces)),
        out_shape=[
            *[jax.ShapeDtypeStruct(shape, BF16)] * 2,
            jax.ShapeDtypeStruct((*shape[:2], 2), jnp.int32),
        ],
        compiler_params=params(*pieces, *pieces),
    )(*pieces, gains)


def assemble_kernel(parts, *refs):
    pieces, outs = refs[:parts], refs[parts:]
    _, share, both = pieces[0].shape
    depth = both // 2
    for r, piece in enumerate(pieces):
        for b, out_ref in enumerate(outs):
            out_ref[:, r * share : (r + 1) * share, :] = piece[:, :, b * depth : (b + 1) * depth]


def assemble(pieces):
    count, share, both = pieces[0].shape
    shape = (count, share * len(pieces), both // 2)
    return pl.pallas_call(
        functools.partial(assemble_kernel, len(pieces)),
        out_shape=[jax.ShapeDtypeStruct(shape, BF16)] * 2,
        compiler_params=params(*pieces, *pieces),
    )(*pieces)


def output_kernel(parts, places, *refs):
    pieces, out_ref = refs[:parts], refs[-1]
    count, share, depth = pieces[0].shape
    for r, piece in enumerate(pieces):
        spot = pl.ds(pl.multiple_of((places[1] ^ r) * share, share), share)
        for j in range(count):
            out_ref[spot, j * depth : (j + 1) * depth] = piece[places[0] ^ j].astype(out_ref.dtype)


def output_rows(places, pieces, dtype):
    pieces = [pieces[r] for r in sorted(pieces)]
    count, share, depth = pieces[0].shape
    shape = (share * len(pieces), count * depth)
    return pl.pallas_call(
        functools.partial(output_kernel, len(pieces)),
        out_shape=jax.ShapeDtypeStruct(shape, dtype),
        grid_spec=pltpu.PrefetchScalarGridSpec(
            num_scalar_prefetch=1,
            grid=(1,),
            in_specs=[whole_spec(one.shape) for one in pieces],
            out_specs=whole_spec(shape),
        ),
        compiler_params=params(*pieces, *pieces),
    )(places, *pieces)


def hidden_kernel(own_ref, gain_ref, *refs):
    came, (hidden_ref, scale_ref, normed_ref) = refs[:-3], refs[-3:]
    depth = own_ref.shape[2]
    squares = 0.0
    for at, one in enumerate(came):
        for b in range(2):
            hidden = own_ref[2 * at + b].astype(F32) + one[:, b * depth : (b + 1) * depth].astype(F32)
            hidden_ref[2 * at + b] = hidden
            squares += jnp.sum(hidden * hidden, axis=1, keepdims=True)
    scale = lax.rsqrt(squares / D + EPSILON)
    scale_ref[...] = scale
    for j in range(2 * len(came)):
        normed_ref[j] = (hidden_ref[j] * scale * gain_ref[j]).astype(BF16)


def hidden_rows(own, gain, came):
    came = [came[k] for k in sorted(came)]
    count, share, depth = own.shape
    return pl.pallas_call(
        hidden_kernel,
        out_shape=[
            jax.ShapeDtypeStruct(own.shape, F32),
            jax.ShapeDtypeStruct((share, 1), F32),
            jax.ShapeDtypeStruct(own.shape, BF16),
        ],
        compiler_params=params(own, own, own, own),
    )(own, gain, *came)


def dispatch_kernel(parts, places, slot_ref, routes_ref, router_ref, up_ref, *refs):
    pieces, (rows_ref, grads_ref, gates_ref) = refs[:parts], refs[parts:]
    count, _, depth = pieces[0].shape
    slots, length = rows_ref.shape[0], slot_ref.shape[1]
    logits = jnp.zeros((EXPERTS, length), F32)
    for j in range(count):
        block = jnp.concatenate([piece[j] for piece in pieces])
        logits += lax.dot_general(
            router_ref[j], block, (((1,), (1,)), ((), ())), preferred_element_type=F32
        )
    kinds = lax.broadcasted_iota(jnp.int32, (EXPERTS, length), 0)
    picked = [
        jnp.sum(jnp.where(kinds == routes_ref[c : c + 1, :], logits, 0.0), axis=0, keepdims=True)
        for c in range(2)
    ]
    top = jnp.maximum(picked[0], picked[1])
    powers = [jnp.exp(one - top) for one in picked]
    gates = [one / (powers[0] + powers[1]) for one in powers]
    slot_at = lax.broadcasted_iota(jnp.int32, (slots, length), 0)
    here = [slot_at == slot_ref[c : c + 1, :] for c in range(2)]
    gate = jnp.where(here[0], gates[0], jnp.where(here[1], gates[1], 0.0))
    gate = jnp.sum(gate, axis=1, keepdims=True)
    place = jnp.where(here[0] | here[1], 1.0, 0.0).astype(BF16)
    for j in range(count):
        lanes = slice(j * depth, (j + 1) * depth)
        block = jnp.concatenate([piece[places[0] ^ j] for piece in pieces])
        rows_ref[:, lanes] = jnp.dot(place, block, preferred_element_type=F32).astype(BF16)
        grads = jnp.dot(place, up_ref[places[0] ^ j], preferred_element_type=F32)
        grads_ref[:, lanes] = (grads * gate).astype(BF16)
    for c in range(2):
        gates_ref[c : c + 1, :] = gates[c]


def dispatch(places, slot, routes, router, up, pieces, slots):
    pieces = [pieces[r] for r in sorted(pieces)]
    operands = (slot, routes, router, up, *pieces)
    shapes = [(slots, D), (slots, D), slot.shape]
    return pl.pallas_call(
        functools.partial(dispatch_kernel, len(pieces)),
        out_shape=[
            jax.ShapeDtypeStruct(shape, dtype) for shape, dtype in zip(shapes, (BF16, BF16, F32))
        ],
        grid_spec=pltpu.PrefetchScalarGridSpec(
            num_scalar_prefetch=1,
            grid=(1,),
            in_specs=[whole_spec(one.shape) for one in operands],
            out_specs=[whole_spec(shape) for shape in shapes],
        ),
        compiler_params=params(up, up, *pieces),
    )(places, *operands)


def combine_kernel(parts, weigh, places, slot_ref, values_ref, *refs):
    extra, outs = refs[: 2 * weigh], refs[2 * weigh :]
    count, share, depth = outs[0].shape
    slots, length = values_ref.shape[0], slot_ref.shape[1]
    slot_at = lax.broadcasted_iota(jnp.int32, (slots, length), 0)
    here = [slot_at == slot_ref[c : c + 1, :] for c in range(2)]
    if weigh:
        gates_ref, grads_ref = extra
        place = jnp.where(
            here[0], gates_ref[0:1, :], jnp.where(here[1], gates_ref[1:2, :], 0.0)
        ).astype(BF16)
        weighted = jnp.sum(
            values_ref[...].astype(F32) * grads_ref[...].astype(F32), axis=1, keepdims=True
        )
        for c in range(2):
            outs[-1][c : c + 1, :] = jnp.sum(
                jnp.where(here[c], weighted, 0.0), axis=0, keepdims=True
            )
    else:
        place = jnp.where(here[0] | here[1], 1.0, 0.0).astype(BF16)
    over_slots = (((0,), (0,)), ((), ()))
    for j in range(count):
        total = lax.dot_general(
            place, values_ref[:, j * depth : (j + 1) * depth], over_slots, preferred_element_type=F32
        ).astype(BF16)
        for r in range(parts):
            outs[r][places[0] ^ j] = total[r * share : (r + 1) * share]


def combine(places, slot, values, parts, count, *extra):
    slots, length = values.shape[0], slot.shape[1]
    shape = (count, length // parts, D // count)
    outs = [jax.ShapeDtypeStruct(shape, BF16)] * parts
    outs += [jax.ShapeDtypeStruct((2, length), F32)] * bool(extra)
    operands = (slot, values, *extra)
    return pl.pallas_call(
        functools.partial(combine_kernel, parts, 1 if extra else 0),
        out_shape=outs,
        grid_spec=pltpu.PrefetchScalarGridSpec(
            num_scalar_prefetch=1,
            grid=(1,),
            in_specs=[whole_spec(one.shape) for one in operands],
            out_specs=[whole_spec(one.shape) for one in outs],
        ),
        compiler_params=params(values, *extra, *outs),
    )(places, *operands)


def map_grads_kernel(n_x, n_sides, *refs):
    x_refs, routes_refs = refs[:n_x], refs[n_x : n_x + n_sides]
    outs, (turned, picked) = refs[-2 - n_x // n_sides : -2], refs[-2:]
    rows = refs[n_x + n_sides : -2 - n_x // n_sides]
    count, length, depth = x_refs[0].shape
    blocks = n_x // n_sides
    for at, x_ref in enumerate(x_refs):
        side, block = at // blocks, at % blocks
        for k in range(count):
            here = slice((side * count + k) * length, (side * count + k + 1) * length)
            turned[block * depth : (block + 1) * depth, here] = x_ref[k].T
    for kind in range(EA):
        for side, routes_ref in enumerate(routes_refs):
            for k in range(count):
                ones = one_of(routes_ref[k], kind)
                at = side * count + k
                picked[at * length : (at + 1) * length, :] = (
                    rows[2 * at][...] * ones[:, 0:1] + rows[2 * at + 1][...] * ones[:, 1:2]
                )
        for block, out_ref in enumerate(outs):
            out_ref[:, kind, :] = jnp.dot(
                turned[block * depth : (block + 1) * depth, :],
                picked[...],
                preferred_element_type=F32,
            ).astype(out_ref.dtype)


def map_grads(sides, routes, rows, dtypes):
    xs = [x for side in sides for x in side]
    count, length, depth = xs[0].shape
    width = rows[0].shape[1]
    total = len(sides) * count * length
    return pl.pallas_call(
        functools.partial(map_grads_kernel, len(xs), len(sides)),
        out_shape=[jax.ShapeDtypeStruct((depth, EA, width), dtype) for dtype in dtypes],
        scratch_shapes=[
            pltpu.VMEM((depth * len(dtypes), total), BF16),
            pltpu.VMEM((total, width), BF16),
        ],
        compiler_params=pltpu.CompilerParams(vmem_limit_bytes=VMEM),
    )(*xs, *routes, *rows)


def turn(values, cosine, sine):
    return values * cosine + pltpu.roll(values, HEAD_DIM // 2, 1) * sine


def rows_kernel(x_ref, *refs):
    pieces, out_ref = refs[:-1], refs[-1]
    total = jnp.zeros(out_ref.shape, F32)
    for j, piece in enumerate(pieces):
        total += jnp.dot(x_ref[j], piece[...], preferred_element_type=F32)
    out_ref[...] = total


def dense_rows(x, pieces):
    _, length, depth = x.shape
    width = pieces[0].shape[1]
    return pl.pallas_call(
        rows_kernel,
        out_shape=jax.ShapeDtypeStruct((length, width), F32),
        compiler_params=params(x, *pieces),
    )(x, *pieces)


def rows_back_kernel(drows_ref, *refs):
    pieces, out_ref = refs[:-1], refs[-1]
    parts, share = out_ref.shape[0], out_ref.shape[2]
    for j, piece in enumerate(pieces):
        total = lax.dot_general(
            drows_ref[...], piece[...], (((1,), (1,)), ((), ())), preferred_element_type=F32
        ).astype(BF16)
        for r in range(parts):
            out_ref[r, j] = total[r * share : (r + 1) * share]


def dense_rows_back(drows, pieces, parts):
    length, width = drows.shape
    depth = pieces[0].shape[0]
    shape = (parts, len(pieces), length // parts, depth)
    return pl.pallas_call(
        rows_back_kernel,
        out_shape=jax.ShapeDtypeStruct(shape, BF16),
        compiler_params=params(drows, *pieces),
    )(drows, *pieces)


def dense_grad_kernel(which, x_ref, y_ref, rows_ref, other_ref, *outs):
    for at, (k, out_ref) in enumerate(zip(which, outs)):
        total = jnp.dot(x_ref[k].T, rows_ref[...], preferred_element_type=F32)
        total += jnp.dot(y_ref[k // 2].T, other_ref[...], preferred_element_type=F32)
        out_ref[...] = total.astype(out_ref.dtype)


def dense_grad(which, x, y, rows, other, dtype):
    _, length, depth = x.shape
    width = rows.shape[1]
    outs = [jax.ShapeDtypeStruct((depth, width), dtype)] * len(which)
    return pl.pallas_call(
        functools.partial(dense_grad_kernel, which),
        out_shape=outs,
        compiler_params=params(x, y, rows, other, *outs),
    )(x, y, rows, other)


def allowed_of(seg_col, seg_row, place_col, place_row):
    return (seg_col[...] == seg_row[...]) & (place_row[...] <= place_col[...])


def attend_kernel(
    first_ref, second_ref, dense_ref, gates_ref, cos_ref, sin_ref, seg_col, seg_row, place_col, place_row, query_ref, key_ref, lse_ref, mixed_ref, *send_refs
):
    width = first_ref.shape[1]
    heads = width // HEAD_DIM
    cosine, sine = cos_ref[...], sin_ref[...]
    allowed = allowed_of(seg_col, seg_row, place_col, place_row)
    for head in range(heads):
        at = head * HEAD_DIM
        key_at, value_at = slice(at, at + HEAD_DIM), slice(width + at, width + at + HEAD_DIM)
        key = turn(dense_ref[:, key_at], cosine, sine).astype(BF16)
        value = dense_ref[:, value_at].astype(BF16)
        key_ref[:, key_at] = key
        key_ref[:, value_at] = value
        for choice, raw_ref in enumerate((first_ref, second_ref)):
            here = slice(choice * width + at, choice * width + at + HEAD_DIM)
            query = turn(raw_ref[:, key_at], cosine, sine).astype(BF16)
            query_ref[:, here] = query
            scores = lax.dot_general(
                query, key, (((1,), (1,)), ((), ())), preferred_element_type=F32
            ) * HEAD_DIM ** (-0.5)
            scores = jnp.where(allowed, scores, -1e30)
            top = jnp.max(scores, axis=1, keepdims=True)
            lse = top + jnp.log(jnp.sum(jnp.exp(scores - top), axis=1, keepdims=True))
            lse_ref[:, choice * heads + head : choice * heads + head + 1] = lse
            probs = jnp.exp(scores - lse).astype(BF16)
            mixed = jnp.dot(probs, value, preferred_element_type=F32).astype(BF16)
            mixed_ref[:, here] = mixed
            send_refs[choice][:, key_at] = (
                mixed.astype(F32) * gates_ref[:, choice : choice + 1]
            ).astype(BF16)


def attend(raw, dense, gates, tables):
    length, width = raw[0].shape
    return pl.pallas_call(
        attend_kernel,
        out_shape=[
            jax.ShapeDtypeStruct((length, 2 * width), BF16),
            jax.ShapeDtypeStruct((length, 2 * width), BF16),
            jax.ShapeDtypeStruct((length, 2 * width // HEAD_DIM), F32),
            jax.ShapeDtypeStruct((length, 2 * width), BF16),
            *[jax.ShapeDtypeStruct((length, width), BF16)] * 2,
        ],
        compiler_params=pltpu.CompilerParams(vmem_limit_bytes=24 << 20),
    )(*raw, dense, gates, *tables)


def attend_back_kernel(
    query_ref, key_ref, lse_ref, mixed_ref, first_ref, second_ref, gates_ref, cos_ref, sin_ref, seg_col, seg_row, place_col, place_row, *refs
):
    dquery_refs, (dkey_ref, dgates_ref) = refs[:2], refs[2:]
    length = query_ref.shape[0]
    width = query_ref.shape[1] // 2
    heads = width // HEAD_DIM
    cosine, sine = cos_ref[...], sin_ref[...]
    allowed = allowed_of(seg_col, seg_row, place_col, place_row)
    turned = (((1,), (1,)), ((), ()))
    dgates = [jnp.zeros((length, 1), F32), jnp.zeros((length, 1), F32)]
    for head in range(heads):
        at = head * HEAD_DIM
        key_at, value_at = slice(at, at + HEAD_DIM), slice(width + at, width + at + HEAD_DIM)
        key, value = key_ref[:, key_at], key_ref[:, value_at]
        dkey = jnp.zeros((length, HEAD_DIM), F32)
        dvalue = jnp.zeros((length, HEAD_DIM), F32)
        for choice, pull_ref in enumerate((first_ref, second_ref)):
            here = slice(choice * width + at, choice * width + at + HEAD_DIM)
            query, pull = query_ref[:, here], pull_ref[:, key_at]
            dgates[choice] += jnp.sum(mixed_ref[:, here].astype(F32) * pull, axis=1, keepdims=True)
            dmixed = (pull * gates_ref[:, choice : choice + 1]).astype(BF16)
            scores = lax.dot_general(query, key, turned, preferred_element_type=F32) * HEAD_DIM ** (-0.5)
            scores = jnp.where(allowed, scores, -1e30)
            probs = jnp.exp(scores - lse_ref[:, choice * heads + head : choice * heads + head + 1])
            dprobs = lax.dot_general(dmixed, value, turned, preferred_element_type=F32)
            inner = jnp.sum(probs * dprobs, axis=1, keepdims=True)
            dscores = (probs * (dprobs - inner)).astype(BF16)
            dquery = jnp.dot(dscores, key, preferred_element_type=F32) * HEAD_DIM ** (-0.5)
            dquery_refs[choice][:, key_at] = turn(dquery, cosine, -sine).astype(BF16)
            dkey += jnp.dot(dscores.T, query, preferred_element_type=F32)
            dvalue += jnp.dot(probs.astype(BF16).T, dmixed, preferred_element_type=F32)
        dkey_ref[:, key_at] = turn(dkey * HEAD_DIM ** (-0.5), cosine, -sine).astype(BF16)
        dkey_ref[:, value_at] = dvalue.astype(BF16)
    for choice in range(2):
        dgates_ref[:, choice : choice + 1] = dgates[choice]


def attend_back(query, key, lse, mixed, pull, gates, tables):
    length, width = pull[0].shape
    return pl.pallas_call(
        attend_back_kernel,
        out_shape=[
            *[jax.ShapeDtypeStruct((length, width), BF16)] * 2,
            jax.ShapeDtypeStruct(key.shape, BF16),
            jax.ShapeDtypeStruct(gates.shape, F32),
        ],
        compiler_params=pltpu.CompilerParams(vmem_limit_bytes=24 << 20),
    )(query, key, lse, mixed, *pull, gates, *tables)


def angles(places):
    half = HEAD_DIM // 2
    freqs = ROTARY_BASE ** (-(jnp.arange(half, dtype=F32) * 2.0 / HEAD_DIM))
    phase = places.astype(F32)[:, None] * freqs[None, :]
    cosine, sine = jnp.cos(phase), jnp.sin(phase)
    return jnp.concatenate([cosine, cosine], axis=1), jnp.concatenate([-sine, sine], axis=1)


def chosen_of(routes, kinds):
    return (routes[:, :, None] == jnp.arange(kinds, dtype=jnp.int32)).astype(F32)


def pair_gates(logits, chosen):
    return jax.nn.softmax(jnp.sum(logits[:, None, :] * chosen, axis=2), axis=-1)


def logit_grad(gates, weighted, chosen):
    inner = weighted - gates * jnp.sum(weighted, axis=1, keepdims=True)
    return jnp.sum(inner[:, :, None] * chosen, axis=1)


def slots_of(chosen, quarter):
    named = jnp.sum(chosen, axis=1)
    rows = named.shape[0]
    before = (jnp.arange(rows)[:, None] > jnp.arange(rows)[None, :]).astype(F32)
    rank = jnp.sum((before @ named)[:, None, :] * chosen, axis=2).astype(jnp.int32)
    kind = jnp.sum(chosen * jnp.arange(chosen.shape[2], dtype=F32), axis=2).astype(jnp.int32)
    return rank // quarter, kind * quarter + rank % quarter


def body(
    tokens,
    cotangent,
    segment_ids,
    routes_att,
    routes_mlp,
    gain_att,
    router_att,
    w_query,
    w_key,
    w_value,
    w_output,
    gain_mlp,
    router_mlp,
    w_gate,
    w_up,
    w_down,
):
    parts = lax.axis_size("tensor")
    devices = lax.axis_size("expert")
    group = devices // EXPERTS
    length = tokens.shape[0]
    share = length // parts
    quarter = CAP // parts
    depth = gain_att.shape[0]
    width = w_key.shape[1]
    me = lax.axis_index("expert")
    part = lax.axis_index("tensor")
    places = jnp.stack([me, part]).astype(jnp.int32)
    order = part ^ jnp.arange(parts)
    far = bits_of("expert")[:-1]
    mine = range(0, devices, 2)

    def by_part(values):
        shaped = values.reshape(parts, share, *values.shape[1:])
        return jnp.take(shaped, order, axis=0).reshape(values.shape)

    def gather_far(first, second):
        halves = [gather_pieces(one, "expert", far) for one in (first, second)]
        return {k: (halves[0][k], halves[1][k]) for k in mine}

    def pair(values):
        return hop(values, "expert", 1)

    own_meta = jnp.concatenate(
        [gain_att, gain_mlp, router_att.T.reshape(-1), router_mlp.T.reshape(-1)]
    ).reshape(18, depth)
    pair_meta = pair(own_meta)

    def swap(sent):
        return jnp.stack([hop(one, "expert", k) if k else one for k, one in zip(mine, sent)])

    by_block = swap([jnp.stack([own_meta, pair_meta])] * len(mine)).reshape(devices, 18, depth)
    gain_one, gain_two = by_block[:, :1].astype(F32), by_block[:, 1:2].astype(F32)
    route_one, route_two = by_block[:, 2 : 2 + EA], by_block[:, 2 + EA :]

    belt = []

    def on_belt(values):
        belt.append(pair(after(values, belt[-2]) if len(belt) > 1 else values))
        return belt[-1]

    query_own = w_query.transpose(1, 0, 2)
    query_pair = [on_belt(query_own[at : at + 2]) for at in range(0, EA, 2)]
    query_ws = [[query_own], query_pair]

    blocks, scale_one, chunks = pack(places, tokens, routes_att, parts, devices)
    chunks[1] = after(chunks[1], by_block)
    came = after(swap(chunks), belt[0])
    token_pieces = gather_pieces(came, "tensor")
    dense_pieces = gather_pieces(
        after(jnp.concatenate([w_key, w_value], axis=1), came), "expert", far
    )
    normed_own, normed_pair, routes_far = unpack(
        [after(token_pieces[r], belt[2]) if r == 3 else token_pieces[r] for r in range(parts)],
        by_block[:2, 0].astype(F32),
    )
    normed_far = [normed_own, normed_pair]
    for k in mine:
        dense_pieces[k ^ 1] = on_belt(dense_pieces[k])
    dense_pieces = [dense_pieces[j] for j in range(devices)]
    normed_blocks = (blocks.astype(F32) * scale_one * gain_one).astype(BF16)
    output_own = after(w_output, normed_own).transpose(1, 0, 2)
    output_pair = [on_belt(output_own[at : at + 2]) for at in range(0, EA, 2)]
    output_ws = [[output_own], output_pair]
    routes_one = by_part(after(routes_att, normed_own))

    chosen_one = chosen_of(routes_one, EA)
    gates_one = pair_gates(
        jnp.einsum("jtd,jkd->tk", normed_blocks, route_one, preferred_element_type=F32), chosen_one
    )

    def project_sum(xs, ws, ties=((), ())):
        late = [k for k in mine if not k & 2]
        early = [k for k in mine if k & 2][::-1]
        found = project(tuple(early), xs, ws, routes_far, BF16)
        rest = project(tuple(late), [after(xs[0], *found, *ties[0]), xs[1]], ws, routes_far, F32)
        sums, came = [], []
        for choice in range(2):
            chunks = dict(zip(early, found[choice::2])) | dict(zip(late, rest[choice::2]))
            total, here = scatter_sum(chunks, "expert", far, BF16)
            sums.append(after(total, *ties[1]))
            came.append(here)
        return sums, rest, came

    raw, started, _ = project_sum(normed_far, query_ws)
    dense_raw = dense_rows(normed_blocks, dense_pieces)
    at_row = (order[:, None] * share + jnp.arange(share)).reshape(-1).astype(jnp.int32)
    at_row = after(at_row, *started)
    segment = by_part(after(segment_ids, *started)[0])
    tables = (*angles(at_row), segment[:, None], segment[None, :], at_row[:, None], at_row[None, :])

    routes_mlp = after(routes_mlp, *started)
    chosen_two = chosen_of(routes_mlp, EXPERTS)
    slot_part, slot = slots_of(chosen_two, quarter)
    slot = by_part(jnp.where(slot_part == part, slot, -1)).T
    routes_two = by_part(routes_mlp).T
    own_chosen = routes_two[:, None, :share] == jnp.arange(EXPERTS, dtype=jnp.int32)[None, :, None]
    own_chosen = own_chosen.astype(F32)
    up = arrange(places, after(cotangent, *started), parts, devices)
    own_up = up[:, :share].astype(F32)
    slots = EXPERTS * quarter

    raw = after(raw, slot, routes_two, own_chosen, up, *tables)
    query, key, lse, mixed, *mixed_sent = attend(raw, dense_raw, gates_one, tables)
    mixed_pieces = gather_far(*mixed_sent)
    branch = to_owners(mixed_pieces, routes_far, output_ws, parts)
    own_tokens = blocks[:, :share]
    hidden, scale_two, own_two = hidden_rows(own_tokens, gain_two, branch)

    rows, dexpert, gates_two = dispatch(
        places, slot, routes_two, route_two, up, gather_pieces(own_two, "tensor"), slots
    )

    def to_experts(values):
        shaped = values.reshape(EXPERTS, 1, quarter, D)
        shaped = jnp.broadcast_to(shaped, (EXPERTS, group, quarter, D)).reshape(devices, quarter, D)
        return lax.all_to_all(shaped, "expert", 0, 0, tiled=True).reshape(devices * quarter, D)

    def back_home(summed):
        summed = summed.astype(BF16).reshape(devices, quarter, D)
        back = lax.all_to_all(summed, "expert", 0, 0, tiled=True)
        back = back.reshape(EXPERTS, group, quarter, D)
        if group > 1:
            back = jnp.sum(back.astype(F32), axis=1).astype(BF16)
        return back.reshape(slots, D)

    turned = (((1,), (1,)), ((), ()))

    def forward(half):
        gate_pre = jnp.dot(half, w_gate[0], preferred_element_type=F32)
        up_pre = jnp.dot(half, w_up[0], preferred_element_type=F32)
        return gate_pre, up_pre, (jax.nn.silu(gate_pre) * up_pre).astype(BF16)

    def backward(half, gate_pre, up_pre):
        dacted = lax.dot_general(half, w_down[0], turned, preferred_element_type=F32)
        sigma = jax.nn.sigmoid(gate_pre)
        dup = (dacted * gate_pre * sigma).astype(BF16)
        dgate = (dacted * up_pre * sigma * (1.0 + gate_pre * (1.0 - sigma))).astype(BF16)
        dinput = lax.dot_general(dgate, w_gate[0], turned, preferred_element_type=F32)
        dinput += lax.dot_general(dup, w_up[0], turned, preferred_element_type=F32)
        return dgate, dup, dinput.astype(BF16)

    assert parts == 4
    came_rows = to_experts(rows)
    far_rows = hop(came_rows, "tensor", 2)
    row_halves = [jnp.concatenate([came_rows, hop(came_rows, "tensor", 1)])]
    pre = [forward(row_halves[0])]
    came_grads = to_experts(after(dexpert, came_rows))
    far_grads = hop(came_grads, "tensor", 2)
    far_rows = after(far_rows, came_grads, pre[0][2])
    row_halves.append(jnp.concatenate([far_rows, hop(far_rows, "tensor", 1)]))
    pre.append(forward(row_halves[1]))
    far_grads = after(far_grads, pre[1][2])
    grad_halves = [
        jnp.concatenate([one, hop(one, "tensor", 1)]) for one in (came_grads, far_grads)
    ]
    expert_part = [
        jnp.dot(acted, w_down[0], preferred_element_type=F32).astype(BF16)
        for _, _, acted in pre[::-1]
    ][::-1]

    def sum_far(half):
        far_chunk, last = jnp.split(half, 2)
        return (far_chunk.astype(F32) + hop(last, "tensor", 1).astype(F32)).astype(BF16)

    def sum_near(half, came):
        chunk, last = jnp.split(half, 2)
        return chunk.astype(F32) + hop(last, "tensor", 1).astype(F32) + came.astype(F32)

    expert_far = sum_far(expert_part[1])
    expert_out = back_home(sum_near(expert_part[0], hop(expert_far, "tensor", 2)))
    back_far = backward(
        after(grad_halves[1], *expert_part), *pre[1][:2]
    )
    input_far = sum_far(back_far[2])
    back_near = backward(
        after(grad_halves[0], input_far), *pre[0][:2]
    )
    dreturned = back_home(sum_near(back_near[2], hop(input_far, "tensor", 2)))

    expert_rows, dout_rows = jnp.concatenate(row_halves), jnp.concatenate(grad_halves)
    acted = jnp.concatenate([one[2] for one in pre])
    dgate = jnp.concatenate([back_near[0], back_far[0]])
    dup = jnp.concatenate([back_near[1], back_far[1]])
    acted, dgate, dup = after((acted, dgate, dup), back_near[2])
    grad_down = jnp.einsum("rf,rd->fd", acted, dout_rows, preferred_element_type=F32)[None]
    grad_gate = jnp.einsum("rd,rf->df", expert_rows, dgate, preferred_element_type=F32)[None]
    grad_up = jnp.einsum("rd,rf->df", expert_rows, dup, preferred_element_type=F32)[None]

    *out_chunks, weighted = combine(places, slot, expert_out, parts, devices, gates_two, dexpert)
    weighted, _ = scatter_sum(
        {r: weighted[:, r * share : (r + 1) * share] for r in range(parts)}, "tensor"
    )
    moe, _ = scatter_sum(dict(enumerate(out_chunks)), "tensor")
    dreturned = after(dreturned, grad_down, grad_gate, grad_up)
    back_chunks = combine(places, slot, dreturned, parts, devices)
    own_gates_two = gates_two[:, :share]
    inner = weighted - own_gates_two * jnp.sum(weighted, axis=0, keepdims=True)
    own_dlogits = jnp.sum(inner[:, None, :] * own_chosen, axis=0)
    dnormed = scatter_sum(dict(enumerate(back_chunks)), "tensor")[0] + jnp.einsum(
        "kt,jkd->jtd", own_dlogits, route_two.astype(F32), precision=PRECISE
    )
    pulled = dnormed * gain_two
    inner_mean = jnp.sum(pulled * hidden, axis=(0, 2), keepdims=True) / D
    dhidden = own_up + scale_two * pulled - hidden * (scale_two * scale_two * scale_two * inner_mean)

    sent = dhidden.astype(BF16)
    up_pieces = gather_pieces(swap(
        [jnp.concatenate([sent[k], sent[k ^ 1]], axis=1) for k in mine]
    ), "tensor")
    dhidden_far = assemble([up_pieces[r] for r in range(parts)])
    pull, started, arrived = project_sum(dhidden_far, output_ws)
    pair_normed = pair(after(normed_far[1], *started))
    pair_blocks = pair(after(normed_blocks[1::2], *started))
    pair_routes = pair(after(routes_far, *started).astype(BF16).transpose(0, 2, 1))
    pair_routes = pair_routes.transpose(0, 2, 1).astype(jnp.int32)
    grad_output, pair_grad = map_grads(
        [[after(dhidden_far[0], *started), dhidden_far[1]]],
        [routes_far],
        [half for k in mine for half in mixed_pieces[k]],
        (F32, BF16),
    )
    pair_grad = pair(pair_grad)
    mixed_out = output_rows(
        places, gather_pieces(after((hidden + moe).astype(BF16), *started), "tensor"), BF16
    )
    def to_features(partial):
        count = partial.shape[0]
        chunks = jnp.take(partial.transpose(1, 0, 2), me ^ jnp.arange(devices), axis=0)[:, None]
        chunks = jnp.broadcast_to(chunks, (devices, parts, count, depth)).reshape(-1, count, depth)
        return jnp.sum(lax.all_to_all(chunks, ("expert", "tensor"), 0, 0, tiled=True), axis=0)

    part_gain_two = jnp.sum(dnormed * hidden * scale_two, axis=1)[None]
    part_route_two = jnp.einsum(
        "kt,jtd->kjd", own_dlogits, own_two.astype(F32), precision=PRECISE
    )

    small_two = to_features(after(jnp.concatenate([part_gain_two, part_route_two]), *started))
    pull = after(pull, small_two, grad_output, pair_normed, pair_blocks)
    *dqueries, ddense, dgates_one = attend_back(query, key, lse, mixed, pull, gates_one, tables)
    pair_dense = pair(ddense)
    dquery_pieces = gather_far(*dqueries)
    pair_dquery = {k: [pair(one) for one in dquery_pieces[k]] for k in mine}
    dnormed_came = to_owners(
        dquery_pieces,
        routes_far,
        query_ws,
        parts,
        ((pair_dense, *pair_dquery[0]), pair_dquery[2]),
    )
    dense_back = dense_rows_back(after(ddense, *dquery_pieces[2]), dense_pieces, parts)
    dense_share, _ = scatter_sum({r: dense_back[r] for r in range(parts)}, "tensor")
    dgates_one, _ = scatter_sum(
        {r: dgates_one[r * share : (r + 1) * share] for r in range(parts)}, "tensor"
    )
    grad_chunks = {}
    for which, dtype in (
        (tuple(k for k in mine if k & 2)[::-1], BF16),
        (tuple(k for k in mine if not k & 2), F32),
    ):
        found = dense_grad(which, normed_blocks, pair_blocks, ddense, pair_dense, dtype)
        grad_chunks.update(zip(which, found))
    grad_dense, dense_came = scatter_sum(grad_chunks, "expert", far, BF16)
    (grad_query,) = map_grads(
        [[normed_far[0]], [pair_normed]],
        [routes_far, pair_routes],
        [half for side in (dquery_pieces, pair_dquery) for k in mine for half in side[k]],
        (F32,),
    )
    grad_key, grad_value = grad_dense[:, :width], grad_dense[:, width:]

    own_gates, own_scale = gates_one[:share], scale_one[:share]
    own_dlogits_one = logit_grad(own_gates, own_gates * dgates_one, chosen_one[:share])
    dnormed_came[0] = after(dnormed_came[0], *pair_dquery[4], *pair_dquery[6])
    whole = jnp.stack(
        [
            dnormed_came[k][:, b * depth : (b + 1) * depth].astype(F32)
            for k in mine
            for b in range(2)
        ]
    )
    dnormed_one = whole + dense_share + jnp.einsum(
        "tk,jkd->jtd", own_dlogits_one, route_one.astype(F32), precision=PRECISE
    )
    pulled_one = dnormed_one * gain_one
    token_rows = own_tokens.astype(F32)
    inner_one = jnp.sum(pulled_one * token_rows, axis=(0, 2), keepdims=True) / D
    own_grad = (
        dhidden
        + own_scale * pulled_one
        - token_rows * (own_scale * own_scale * own_scale * inner_one)
    )
    own_grad = after(own_grad.astype(BF16), *dense_came[:-1])
    grad_pieces = gather_pieces(own_grad, "tensor")
    grad_tokens = output_rows(places, {**grad_pieces, 3: after(grad_pieces[3], grad_dense)}, F32)
    part_gain_one = jnp.sum(dnormed_one * token_rows * own_scale, axis=1)[None]
    part_route_one = jnp.einsum(
        "tk,jtd->kjd", own_dlogits_one, normed_blocks[:, :share].astype(F32), precision=PRECISE
    )

    small_one = to_features(jnp.concatenate([part_gain_one, part_route_one]))
    return (
        mixed_out,
        grad_tokens,
        small_one[0],
        small_one[1:].T,
        grad_query,
        grad_key,
        grad_value,
        grad_output + pair_grad.astype(F32),
        small_two[0],
        small_two[1:].T,
        grad_gate,
        grad_up,
        grad_down,
    )


def solution(mesh):
    in_specs = (
        P("expert", None),
        P("expert", None),
        P("expert", None),
        P("expert", None),
        P("expert", None),
        P("expert"),
        P("expert", None),
        P("expert", None, "tensor"),
        P("expert", "tensor"),
        P("expert", "tensor"),
        P("expert", None, "tensor"),
        P("expert"),
        P("expert", None),
        P("expert", None, "tensor"),
        P("expert", None, "tensor"),
        P("expert", "tensor", None),
    )
    out_specs = (
        P("expert", None),
        P("expert", None),
        P("expert"),
        P("expert", None),
        P("expert", None, "tensor"),
        P("expert", "tensor"),
        P("expert", "tensor"),
        P("expert", None, "tensor"),
        P("expert"),
        P("expert", None),
        P("expert", None, "tensor"),
        P("expert", None, "tensor"),
        P("expert", "tensor", None),
    )
    return jax.shard_map(body, mesh=mesh, in_specs=in_specs, out_specs=out_specs, check_vma=False)
```

```python
import functools

import jax
import jax.numpy as jnp
from jax import lax
from jax.experimental import pallas as pl
from jax.experimental.pallas import tpu as pltpu
from jax.sharding import PartitionSpec as P

D = 2048
HEAD_DIM = 128
EA = 8
EXPERTS = 8
CAP = 96
EPSILON = 1e-05
ROTARY_BASE = 10000.0
VMEM = 56 * 1024 * 1024
F32 = jnp.float32
BF16 = jnp.bfloat16
PRECISE = lax.Precision.HIGHEST


def hop(values, axis, bit):
    size = lax.axis_size(axis)
    return lax.ppermute(values, axis, [(i, i ^ bit) for i in range(size)])


def bits_of(axis):
    size, bits = lax.axis_size(axis), []
    while 1 << len(bits) < size:
        bits.append(1 << len(bits))
    return bits[::-1]


def gather_pieces(values, axis, bits=None):
    pieces = {0: values}
    for bit in bits_of(axis) if bits is None else bits:
        for known in sorted(pieces):
            pieces[known | bit] = hop(pieces[known], axis, bit)
    return pieces


def scatter_sum(chunks, axis, bits=None, sent_as=None):
    held, came = dict(chunks), []
    for bit in (bits_of(axis) if bits is None else bits)[::-1]:
        for k in sorted(held, reverse=True):
            if k & bit:
                sent = held.pop(k)
                came.append(hop(sent.astype(sent_as or sent.dtype), axis, bit))
                held[k ^ bit] = held[k ^ bit].astype(F32) + came[-1].astype(F32)
                if k ^ bit:
                    held[k ^ bit] = held[k ^ bit].astype(sent_as or sent.dtype)
    return held[0], came


def after(values, *earlier):
    return lax.optimization_barrier((values, *earlier))[0]


def whole_spec(shape):
    zeros = (0,) * len(shape)
    return pl.BlockSpec(shape, lambda *_: zeros)


def params(*arrays):
    held = 3 * sum(one.size * one.dtype.itemsize for one in arrays) + (12 << 20)
    return pltpu.CompilerParams(vmem_limit_bytes=min(VMEM, held) if arrays else 16 << 20)


def one_of(routes, kind):
    return (routes == kind).astype(F32).astype(BF16)


def map_of(refs, kind):
    each = EA // len(refs)
    return refs[kind // each][kind % each]


def project_kernel(which, counts, *refs):
    x_refs, refs = refs[: len(counts)], refs[len(counts) :]
    w_refs = []
    for count in counts:
        w_refs.append(refs[:count])
        refs = refs[count:]
    routes_ref, outs = refs[0], refs[1:]
    for at, k in enumerate(which):
        routes = routes_ref[k // 2]
        for choice in range(2):
            total = jnp.zeros(outs[0].shape, F32)
            for x_ref, maps in zip(x_refs, w_refs):
                x = x_ref[k // 2]
                each = EA // len(maps)
                for first, w_ref in zip(range(0, EA, each), maps):
                    spread = jnp.concatenate(
                        [
                            x * one_of(routes[:, choice : choice + 1], kind)
                            for kind in range(first, first + each)
                        ],
                        axis=1,
                    )
                    flat = w_ref[...].reshape(each * x.shape[1], w_ref.shape[2])
                    total += jnp.dot(spread, flat, preferred_element_type=F32)
            outs[2 * at + choice][...] = total.astype(outs[0].dtype)


def project(which, xs, ws, routes, dtype):
    _, length, depth = xs[0].shape
    width = ws[0][0].shape[2]
    outs = [jax.ShapeDtypeStruct((length, width), dtype)] * (2 * len(which))
    maps = [one for side in ws for one in side]
    return pl.pallas_call(
        functools.partial(project_kernel, which, [len(side) for side in ws]),
        out_shape=outs,
        compiler_params=params(*xs, *maps, *outs),
    )(*xs, *maps, routes)


def contract_kernel(which, counts, parts, routes_ref, *refs):
    w_refs = []
    for count in counts:
        w_refs.append(refs[:count])
        refs = refs[count:]
    rows, outs = refs[: 2 * len(which)], refs[2 * len(which) :]
    share, depth = outs[0].shape[1], w_refs[0][0].shape[1]
    turned = (((1,), (1,)), ((), ()))
    for at, k in enumerate(which):
        routes = routes_ref[k // 2]
        first, second = rows[2 * at][...], rows[2 * at + 1][...]
        totals = [jnp.zeros((share * parts, depth), F32)] * len(counts)
        for kind in range(EA):
            ones = one_of(routes, kind)
            picked = first * ones[:, 0:1] + second * ones[:, 1:2]
            totals = [
                total
                + lax.dot_general(picked, map_of(maps, kind), turned, preferred_element_type=F32)
                for total, maps in zip(totals, w_refs)
            ]
        for b, total in enumerate(totals):
            for r in range(parts):
                outs[r][at, :, b * depth : (b + 1) * depth] = total[
                    r * share : (r + 1) * share
                ].astype(outs[r].dtype)


def contract(which, pieces, routes, ws, parts):
    rows = [half for k in which for half in pieces[k]]
    _, length, _ = routes.shape
    depth, width = ws[0][0].shape[1:]
    shape = (len(which), length // parts, depth * len(ws))
    maps = [one for side in ws for one in side]
    return pl.pallas_call(
        functools.partial(contract_kernel, which, [len(side) for side in ws], parts),
        out_shape=[
            jax.ShapeDtypeStruct(shape, BF16 if r % 2 else F32) for r in range(parts)
        ],
        compiler_params=params(*maps, *rows),
    )(routes, *maps, *rows)


def to_owners(pieces, routes, ws, parts, ties=((), (), ())):
    came, order, last = {}, sorted(pieces), ()
    for at_call, which in enumerate((order[:-1], order[-1:])):
        tied = after(routes, *ties[at_call], *last)
        last = contract(tuple(which), pieces, tied, ws, parts)
        summed, _ = scatter_sum(dict(enumerate(last)), "tensor", None, BF16)
        if at_call:
            summed = after(summed, *ties[2])
        for at, k in enumerate(which):
            came[k] = hop(summed[at].astype(BF16), "expert", k) if k else summed[at]
    return came


def arrange_kernel(parts, places, x_ref, out_ref):
    count, length, depth = out_ref.shape
    share = length // parts
    for r in range(parts):
        spot = pl.ds(pl.multiple_of((places[1] ^ r) * share, share), share)
        for j in range(count):
            out_ref[places[0] ^ j, r * share : (r + 1) * share, :] = x_ref[
                spot, j * depth : (j + 1) * depth
            ]


def arrange(places, x, parts, count):
    shape = (count, x.shape[0], x.shape[1] // count)
    return pl.pallas_call(
        functools.partial(arrange_kernel, parts),
        out_shape=jax.ShapeDtypeStruct(shape, BF16),
        grid_spec=pltpu.PrefetchScalarGridSpec(
            num_scalar_prefetch=1,
            grid=(1,),
            in_specs=[whole_spec(x.shape)],
            out_specs=whole_spec(shape),
        ),
        compiler_params=params(x),
    )(places, x)


def pack_kernel(parts, places, x_ref, routes_ref, blocks_ref, scale_ref, *outs):
    count, length, depth = blocks_ref.shape
    share = length // parts
    for r in range(parts):
        spot = pl.ds(pl.multiple_of((places[1] ^ r) * share, share), share)
        rows = slice(r * share, (r + 1) * share)
        squares = jnp.zeros((share, 1), F32)
        for j in range(count):
            block = x_ref[spot, j * depth : (j + 1) * depth]
            blocks_ref[places[0] ^ j, rows, :] = block
            wide = block.astype(F32)
            squares += jnp.sum(wide * wide, axis=1, keepdims=True)
        scale = lax.rsqrt(squares / D + EPSILON)
        scale_ref[rows, :] = scale
        if r == 0:
            high = scale.astype(BF16).astype(F32)
            middle = (scale - high).astype(BF16).astype(F32)
            routes = routes_ref[spot, :].astype(F32)
            columns = [routes[:, 0:1], routes[:, 1:2], high, middle, scale - high - middle]
            lane = lax.broadcasted_iota(jnp.int32, (share, 128), 1)
            extra = jnp.zeros((share, 128), F32)
            for at, column in enumerate(columns):
                extra = jnp.where(lane == at, column, extra)
    for at, out_ref in enumerate(outs):
        for b in range(2):
            out_ref[:, b * depth : (b + 1) * depth] = blocks_ref[2 * at + b, :share, :]
        out_ref[:, 2 * depth :] = extra.astype(BF16)


def pack(places, x, routes, parts, count):
    length, depth = x.shape[0], x.shape[1] // count
    shapes = [(count, length, depth), (length, 1)]
    shapes += [(length // parts, 2 * depth + 128)] * (count // 2)
    types = [BF16, F32] + [BF16] * (count // 2)
    blocks, scale, *chunks = pl.pallas_call(
        functools.partial(pack_kernel, parts),
        out_shape=[jax.ShapeDtypeStruct(*one) for one in zip(shapes, types)],
        grid_spec=pltpu.PrefetchScalarGridSpec(
            num_scalar_prefetch=1,
            grid=(1,),
            in_specs=[whole_spec(x.shape), whole_spec(routes.shape)],
            out_specs=[whole_spec(one) for one in shapes],
        ),
        compiler_params=params(x),
    )(places, x, routes)
    return blocks, scale, chunks


def unpack_kernel(parts, *refs):
    pieces, (gain_ref, *outs, routes_ref) = refs[:parts], refs[parts:]
    share, depth = pieces[0].shape[1], outs[0].shape[2]
    for r, piece in enumerate(pieces):
        rows = slice(r * share, (r + 1) * share)
        for k in range(piece.shape[0]):
            extra = piece[k, :, 2 * depth :].astype(F32)
            scale = extra[:, 2:3] + extra[:, 3:4] + extra[:, 4:5]
            routes_ref[k, rows, :] = extra[:, 0:2].astype(jnp.int32)
            for b, out_ref in enumerate(outs):
                values = piece[k, :, b * depth : (b + 1) * depth].astype(F32)
                out_ref[k, rows, :] = (values * scale * gain_ref[b : b + 1, :]).astype(BF16)


def unpack(pieces, gains):
    count, share, _ = pieces[0].shape
    shape = (count, share * len(pieces), gains.shape[1])
    return pl.pallas_call(
        functools.partial(unpack_kernel, len(pieces)),
        out_shape=[
            *[jax.ShapeDtypeStruct(shape, BF16)] * 2,
            jax.ShapeDtypeStruct((*shape[:2], 2), jnp.int32),
        ],
        compiler_params=params(*pieces, *pieces),
    )(*pieces, gains)


def assemble_kernel(parts, *refs):
    pieces, outs = refs[:parts], refs[parts:]
    _, share, both = pieces[0].shape
    depth = both // 2
    for r, piece in enumerate(pieces):
        for b, out_ref in enumerate(outs):
            out_ref[:, r * share : (r + 1) * share, :] = piece[:, :, b * depth : (b + 1) * depth]


def assemble(pieces):
    count, share, both = pieces[0].shape
    shape = (count, share * len(pieces), both // 2)
    return pl.pallas_call(
        functools.partial(assemble_kernel, len(pieces)),
        out_shape=[jax.ShapeDtypeStruct(shape, BF16)] * 2,
        compiler_params=params(*pieces, *pieces),
    )(*pieces)


def output_kernel(parts, places, *refs):
    pieces, out_ref = refs[:parts], refs[-1]
    count, share, depth = pieces[0].shape
    for r, piece in enumerate(pieces):
        spot = pl.ds(pl.multiple_of((places[1] ^ r) * share, share), share)
        for j in range(count):
            out_ref[spot, j * depth : (j + 1) * depth] = piece[places[0] ^ j].astype(out_ref.dtype)


def output_rows(places, pieces, dtype):
    pieces = [pieces[r] for r in sorted(pieces)]
    count, share, depth = pieces[0].shape
    shape = (share * len(pieces), count * depth)
    return pl.pallas_call(
        functools.partial(output_kernel, len(pieces)),
        out_shape=jax.ShapeDtypeStruct(shape, dtype),
        grid_spec=pltpu.PrefetchScalarGridSpec(
            num_scalar_prefetch=1,
            grid=(1,),
            in_specs=[whole_spec(one.shape) for one in pieces],
            out_specs=whole_spec(shape),
        ),
        compiler_params=params(*pieces, *pieces),
    )(places, *pieces)


def hidden_kernel(own_ref, gain_ref, *refs):
    came, (hidden_ref, scale_ref, normed_ref) = refs[:-3], refs[-3:]
    depth = own_ref.shape[2]
    squares = 0.0
    for at, one in enumerate(came):
        for b in range(2):
            hidden = own_ref[2 * at + b].astype(F32) + one[:, b * depth : (b + 1) * depth].astype(F32)
            hidden_ref[2 * at + b] = hidden
            squares += jnp.sum(hidden * hidden, axis=1, keepdims=True)
    scale = lax.rsqrt(squares / D + EPSILON)
    scale_ref[...] = scale
    for j in range(2 * len(came)):
        normed_ref[j] = (hidden_ref[j] * scale * gain_ref[j]).astype(BF16)


def hidden_rows(own, gain, came):
    came = [came[k] for k in sorted(came)]
    count, share, depth = own.shape
    return pl.pallas_call(
        hidden_kernel,
        out_shape=[
            jax.ShapeDtypeStruct(own.shape, F32),
            jax.ShapeDtypeStruct((share, 1), F32),
            jax.ShapeDtypeStruct(own.shape, BF16),
        ],
        compiler_params=params(own, own, own, own),
    )(own, gain, *came)


def dispatch_kernel(parts, places, slot_ref, routes_ref, router_ref, up_ref, *refs):
    pieces, (rows_ref, grads_ref, gates_ref) = refs[:parts], refs[parts:]
    count, _, depth = pieces[0].shape
    slots, length = rows_ref.shape[0], slot_ref.shape[1]
    logits = jnp.zeros((EXPERTS, length), F32)
    for j in range(count):
        block = jnp.concatenate([piece[j] for piece in pieces])
        logits += lax.dot_general(
            router_ref[j], block, (((1,), (1,)), ((), ())), preferred_element_type=F32
        )
    kinds = lax.broadcasted_iota(jnp.int32, (EXPERTS, length), 0)
    picked = [
        jnp.sum(jnp.where(kinds == routes_ref[c : c + 1, :], logits, 0.0), axis=0, keepdims=True)
        for c in range(2)
    ]
    top = jnp.maximum(picked[0], picked[1])
    powers = [jnp.exp(one - top) for one in picked]
    gates = [one / (powers[0] + powers[1]) for one in powers]
    slot_at = lax.broadcasted_iota(jnp.int32, (slots, length), 0)
    here = [slot_at == slot_ref[c : c + 1, :] for c in range(2)]
    gate = jnp.where(here[0], gates[0], jnp.where(here[1], gates[1], 0.0))
    gate = jnp.sum(gate, axis=1, keepdims=True)
    place = jnp.where(here[0] | here[1], 1.0, 0.0).astype(BF16)
    for j in range(count):
        lanes = slice(j * depth, (j + 1) * depth)
        block = jnp.concatenate([piece[places[0] ^ j] for piece in pieces])
        rows_ref[:, lanes] = jnp.dot(place, block, preferred_element_type=F32).astype(BF16)
        grads = jnp.dot(place, up_ref[places[0] ^ j], preferred_element_type=F32)
        grads_ref[:, lanes] = (grads * gate).astype(BF16)
    for c in range(2):
        gates_ref[c : c + 1, :] = gates[c]


def dispatch(places, slot, routes, router, up, pieces, slots):
    pieces = [pieces[r] for r in sorted(pieces)]
    operands = (slot, routes, router, up, *pieces)
    shapes = [(slots, D), (slots, D), slot.shape]
    return pl.pallas_call(
        functools.partial(dispatch_kernel, len(pieces)),
        out_shape=[
            jax.ShapeDtypeStruct(shape, dtype) for shape, dtype in zip(shapes, (BF16, BF16, F32))
        ],
        grid_spec=pltpu.PrefetchScalarGridSpec(
            num_scalar_prefetch=1,
            grid=(1,),
            in_specs=[whole_spec(one.shape) for one in operands],
            out_specs=[whole_spec(shape) for shape in shapes],
        ),
        compiler_params=params(up, up, *pieces),
    )(places, *operands)


def combine_kernel(parts, weigh, places, slot_ref, values_ref, *refs):
    extra, outs = refs[: 2 * weigh], refs[2 * weigh :]
    count, share, depth = outs[0].shape
    slots, length = values_ref.shape[0], slot_ref.shape[1]
    slot_at = lax.broadcasted_iota(jnp.int32, (slots, length), 0)
    here = [slot_at == slot_ref[c : c + 1, :] for c in range(2)]
    if weigh:
        gates_ref, grads_ref = extra
        place = jnp.where(
            here[0], gates_ref[0:1, :], jnp.where(here[1], gates_ref[1:2, :], 0.0)
        ).astype(BF16)
        weighted = jnp.sum(
            values_ref[...].astype(F32) * grads_ref[...].astype(F32), axis=1, keepdims=True
        )
        for c in range(2):
            outs[-1][c : c + 1, :] = jnp.sum(
                jnp.where(here[c], weighted, 0.0), axis=0, keepdims=True
            )
    else:
        place = jnp.where(here[0] | here[1], 1.0, 0.0).astype(BF16)
    over_slots = (((0,), (0,)), ((), ()))
    for j in range(count):
        total = lax.dot_general(
            place, values_ref[:, j * depth : (j + 1) * depth], over_slots, preferred_element_type=F32
        ).astype(BF16)
        for r in range(parts):
            outs[r][places[0] ^ j] = total[r * share : (r + 1) * share]


def combine(places, slot, values, parts, count, *extra):
    slots, length = values.shape[0], slot.shape[1]
    shape = (count, length // parts, D // count)
    outs = [jax.ShapeDtypeStruct(shape, BF16)] * parts
    outs += [jax.ShapeDtypeStruct((2, length), F32)] * bool(extra)
    operands = (slot, values, *extra)
    return pl.pallas_call(
        functools.partial(combine_kernel, parts, 1 if extra else 0),
        out_shape=outs,
        grid_spec=pltpu.PrefetchScalarGridSpec(
            num_scalar_prefetch=1,
            grid=(1,),
            in_specs=[whole_spec(one.shape) for one in operands],
            out_specs=[whole_spec(one.shape) for one in outs],
        ),
        compiler_params=params(values, *extra, *outs),
    )(places, *operands)


def map_grads_kernel(n_x, n_sides, *refs):
    x_refs, routes_refs = refs[:n_x], refs[n_x : n_x + n_sides]
    outs, (turned, picked) = refs[-2 - n_x // n_sides : -2], refs[-2:]
    rows = refs[n_x + n_sides : -2 - n_x // n_sides]
    count, length, depth = x_refs[0].shape
    blocks = n_x // n_sides
    for at, x_ref in enumerate(x_refs):
        side, block = at // blocks, at % blocks
        for k in range(count):
            here = slice((side * count + k) * length, (side * count + k + 1) * length)
            turned[block * depth : (block + 1) * depth, here] = x_ref[k].T
    for kind in range(EA):
        for side, routes_ref in enumerate(routes_refs):
            for k in range(count):
                ones = one_of(routes_ref[k], kind)
                at = side * count + k
                picked[at * length : (at + 1) * length, :] = (
                    rows[2 * at][...] * ones[:, 0:1] + rows[2 * at + 1][...] * ones[:, 1:2]
                )
        for block, out_ref in enumerate(outs):
            out_ref[:, kind, :] = jnp.dot(
                turned[block * depth : (block + 1) * depth, :],
                picked[...],
                preferred_element_type=F32,
            ).astype(out_ref.dtype)


def map_grads(sides, routes, rows, dtypes):
    xs = [x for side in sides for x in side]
    count, length, depth = xs[0].shape
    width = rows[0].shape[1]
    total = len(sides) * count * length
    return pl.pallas_call(
        functools.partial(map_grads_kernel, len(xs), len(sides)),
        out_shape=[jax.ShapeDtypeStruct((depth, EA, width), dtype) for dtype in dtypes],
        scratch_shapes=[
            pltpu.VMEM((depth * len(dtypes), total), BF16),
            pltpu.VMEM((total, width), BF16),
        ],
        compiler_params=pltpu.CompilerParams(vmem_limit_bytes=VMEM),
    )(*xs, *routes, *rows)


def turn(values, cosine, sine):
    return values * cosine + pltpu.roll(values, HEAD_DIM // 2, 1) * sine


def rows_kernel(x_ref, *refs):
    pieces, out_ref = refs[:-1], refs[-1]
    total = jnp.zeros(out_ref.shape, F32)
    for j, piece in enumerate(pieces):
        total += jnp.dot(x_ref[j], piece[...], preferred_element_type=F32)
    out_ref[...] = total


def dense_rows(x, pieces):
    _, length, depth = x.shape
    width = pieces[0].shape[1]
    return pl.pallas_call(
        rows_kernel,
        out_shape=jax.ShapeDtypeStruct((length, width), F32),
        compiler_params=params(x, *pieces),
    )(x, *pieces)


def rows_back_kernel(drows_ref, *refs):
    pieces, out_ref = refs[:-1], refs[-1]
    parts, share = out_ref.shape[0], out_ref.shape[2]
    for j, piece in enumerate(pieces):
        total = lax.dot_general(
            drows_ref[...], piece[...], (((1,), (1,)), ((), ())), preferred_element_type=F32
        ).astype(BF16)
        for r in range(parts):
            out_ref[r, j] = total[r * share : (r + 1) * share]


def dense_rows_back(drows, pieces, parts):
    length, width = drows.shape
    depth = pieces[0].shape[0]
    shape = (parts, len(pieces), length // parts, depth)
    return pl.pallas_call(
        rows_back_kernel,
        out_shape=jax.ShapeDtypeStruct(shape, BF16),
        compiler_params=params(drows, *pieces),
    )(drows, *pieces)


def dense_grad_kernel(n_x, *refs):
    x_refs, outs = refs[:n_x], refs[-n_x:]
    rows = refs[n_x:-n_x]
    for x_ref, out_ref in zip(x_refs, outs):
        total = jnp.zeros(out_ref.shape, F32)
        for at, one in enumerate(rows):
            total += jnp.dot(x_ref[at].T, one[...], preferred_element_type=F32)
        out_ref[...] = total.astype(out_ref.dtype)


def dense_grad(xs, rows, dtypes):
    depth, width = xs[0].shape[2], rows[0].shape[1]
    return pl.pallas_call(
        functools.partial(dense_grad_kernel, len(xs)),
        out_shape=[jax.ShapeDtypeStruct((depth, width), dtype) for dtype in dtypes],
        compiler_params=params(*xs, *rows),
    )(*xs, *rows)


def allowed_of(seg_col, seg_row, place_col, place_row):
    return (seg_col[...] == seg_row[...]) & (place_row[...] <= place_col[...])


def attend_kernel(
    first_ref, second_ref, dense_ref, gates_ref, cos_ref, sin_ref, seg_col, seg_row, place_col, place_row, query_ref, key_ref, lse_ref, mixed_ref, *send_refs
):
    width = first_ref.shape[1]
    heads = width // HEAD_DIM
    cosine, sine = cos_ref[...], sin_ref[...]
    allowed = allowed_of(seg_col, seg_row, place_col, place_row)
    for head in range(heads):
        at = head * HEAD_DIM
        key_at, value_at = slice(at, at + HEAD_DIM), slice(width + at, width + at + HEAD_DIM)
        key = turn(dense_ref[:, key_at], cosine, sine).astype(BF16)
        value = dense_ref[:, value_at].astype(BF16)
        key_ref[:, key_at] = key
        key_ref[:, value_at] = value
        for choice, raw_ref in enumerate((first_ref, second_ref)):
            here = slice(choice * width + at, choice * width + at + HEAD_DIM)
            query = turn(raw_ref[:, key_at], cosine, sine).astype(BF16)
            query_ref[:, here] = query
            scores = lax.dot_general(
                query, key, (((1,), (1,)), ((), ())), preferred_element_type=F32
            ) * HEAD_DIM ** (-0.5)
            scores = jnp.where(allowed, scores, -1e30)
            top = jnp.max(scores, axis=1, keepdims=True)
            lse = top + jnp.log(jnp.sum(jnp.exp(scores - top), axis=1, keepdims=True))
            lse_ref[:, choice * heads + head : choice * heads + head + 1] = lse
            probs = jnp.exp(scores - lse).astype(BF16)
            mixed = jnp.dot(probs, value, preferred_element_type=F32).astype(BF16)
            mixed_ref[:, here] = mixed
            send_refs[choice][:, key_at] = (
                mixed.astype(F32) * gates_ref[:, choice : choice + 1]
            ).astype(BF16)


def attend(raw, dense, gates, tables):
    length, width = raw[0].shape
    return pl.pallas_call(
        attend_kernel,
        out_shape=[
            jax.ShapeDtypeStruct((length, 2 * width), BF16),
            jax.ShapeDtypeStruct((length, 2 * width), BF16),
            jax.ShapeDtypeStruct((length, 2 * width // HEAD_DIM), F32),
            jax.ShapeDtypeStruct((length, 2 * width), BF16),
            *[jax.ShapeDtypeStruct((length, width), BF16)] * 2,
        ],
        compiler_params=pltpu.CompilerParams(vmem_limit_bytes=24 << 20),
    )(*raw, dense, gates, *tables)


def attend_back_kernel(
    query_ref, key_ref, lse_ref, mixed_ref, first_ref, second_ref, gates_ref, cos_ref, sin_ref, seg_col, seg_row, place_col, place_row, *refs
):
    dquery_refs, (dkey_ref, dgates_ref) = refs[:2], refs[2:]
    length = query_ref.shape[0]
    width = query_ref.shape[1] // 2
    heads = width // HEAD_DIM
    cosine, sine = cos_ref[...], sin_ref[...]
    allowed = allowed_of(seg_col, seg_row, place_col, place_row)
    turned = (((1,), (1,)), ((), ()))
    dgates = [jnp.zeros((length, 1), F32), jnp.zeros((length, 1), F32)]
    for head in range(heads):
        at = head * HEAD_DIM
        key_at, value_at = slice(at, at + HEAD_DIM), slice(width + at, width + at + HEAD_DIM)
        key, value = key_ref[:, key_at], key_ref[:, value_at]
        dkey = jnp.zeros((length, HEAD_DIM), F32)
        dvalue = jnp.zeros((length, HEAD_DIM), F32)
        for choice, pull_ref in enumerate((first_ref, second_ref)):
            here = slice(choice * width + at, choice * width + at + HEAD_DIM)
            query, pull = query_ref[:, here], pull_ref[:, key_at]
            dgates[choice] += jnp.sum(mixed_ref[:, here].astype(F32) * pull, axis=1, keepdims=True)
            dmixed = (pull * gates_ref[:, choice : choice + 1]).astype(BF16)
            scores = lax.dot_general(query, key, turned, preferred_element_type=F32) * HEAD_DIM ** (-0.5)
            scores = jnp.where(allowed, scores, -1e30)
            probs = jnp.exp(scores - lse_ref[:, choice * heads + head : choice * heads + head + 1])
            dprobs = lax.dot_general(dmixed, value, turned, preferred_element_type=F32)
            inner = jnp.sum(probs * dprobs, axis=1, keepdims=True)
            dscores = (probs * (dprobs - inner)).astype(BF16)
            dquery = jnp.dot(dscores, key, preferred_element_type=F32) * HEAD_DIM ** (-0.5)
            dquery_refs[choice][:, key_at] = turn(dquery, cosine, -sine).astype(BF16)
            dkey += jnp.dot(dscores.T, query, preferred_element_type=F32)
            dvalue += jnp.dot(probs.astype(BF16).T, dmixed, preferred_element_type=F32)
        dkey_ref[:, key_at] = turn(dkey * HEAD_DIM ** (-0.5), cosine, -sine).astype(BF16)
        dkey_ref[:, value_at] = dvalue.astype(BF16)
    for choice in range(2):
        dgates_ref[:, choice : choice + 1] = dgates[choice]


def attend_back(query, key, lse, mixed, pull, gates, tables):
    length, width = pull[0].shape
    return pl.pallas_call(
        attend_back_kernel,
        out_shape=[
            *[jax.ShapeDtypeStruct((length, width), BF16)] * 2,
            jax.ShapeDtypeStruct(key.shape, BF16),
            jax.ShapeDtypeStruct(gates.shape, F32),
        ],
        compiler_params=pltpu.CompilerParams(vmem_limit_bytes=24 << 20),
    )(query, key, lse, mixed, *pull, gates, *tables)


def angles(places):
    half = HEAD_DIM // 2
    freqs = ROTARY_BASE ** (-(jnp.arange(half, dtype=F32) * 2.0 / HEAD_DIM))
    phase = places.astype(F32)[:, None] * freqs[None, :]
    cosine, sine = jnp.cos(phase), jnp.sin(phase)
    return jnp.concatenate([cosine, cosine], axis=1), jnp.concatenate([-sine, sine], axis=1)


def chosen_of(routes, kinds):
    return (routes[:, :, None] == jnp.arange(kinds, dtype=jnp.int32)).astype(F32)


def pair_gates(logits, chosen):
    return jax.nn.softmax(jnp.sum(logits[:, None, :] * chosen, axis=2), axis=-1)


def logit_grad(gates, weighted, chosen):
    inner = weighted - gates * jnp.sum(weighted, axis=1, keepdims=True)
    return jnp.sum(inner[:, :, None] * chosen, axis=1)


def slots_of(chosen, quarter):
    named = jnp.sum(chosen, axis=1)
    rows = named.shape[0]
    before = (jnp.arange(rows)[:, None] > jnp.arange(rows)[None, :]).astype(F32)
    rank = jnp.sum((before @ named)[:, None, :] * chosen, axis=2).astype(jnp.int32)
    kind = jnp.sum(chosen * jnp.arange(chosen.shape[2], dtype=F32), axis=2).astype(jnp.int32)
    return rank // quarter, kind * quarter + rank % quarter


def body(
    tokens,
    cotangent,
    segment_ids,
    routes_att,
    routes_mlp,
    gain_att,
    router_att,
    w_query,
    w_key,
    w_value,
    w_output,
    gain_mlp,
    router_mlp,
    w_gate,
    w_up,
    w_down,
):
    parts = lax.axis_size("tensor")
    devices = lax.axis_size("expert")
    group = devices // EXPERTS
    length = tokens.shape[0]
    share = length // parts
    quarter = CAP // parts
    depth = gain_att.shape[0]
    width = w_key.shape[1]
    me = lax.axis_index("expert")
    part = lax.axis_index("tensor")
    places = jnp.stack([me, part]).astype(jnp.int32)
    order = part ^ jnp.arange(parts)
    far = bits_of("expert")[:-1]
    mine = range(0, devices, 2)

    def by_part(values):
        shaped = values.reshape(parts, share, *values.shape[1:])
        return jnp.take(shaped, order, axis=0).reshape(values.shape)

    def gather_far(first, second):
        halves = [gather_pieces(one, "expert", far) for one in (first, second)]
        return {k: (halves[0][k], halves[1][k]) for k in mine}

    def pair(values):
        return hop(values, "expert", 1)

    own_meta = jnp.concatenate(
        [gain_att, gain_mlp, router_att.T.reshape(-1), router_mlp.T.reshape(-1)]
    ).reshape(18, depth)
    pair_meta = pair(own_meta)

    def swap(sent):
        return jnp.stack([hop(one, "expert", k) if k else one for k, one in zip(mine, sent)])

    by_block = swap([jnp.stack([own_meta, pair_meta])] * len(mine)).reshape(devices, 18, depth)
    gain_one, gain_two = by_block[:, :1].astype(F32), by_block[:, 1:2].astype(F32)
    route_one, route_two = by_block[:, 2 : 2 + EA], by_block[:, 2 + EA :]

    belt = []

    def on_belt(values):
        belt.append(pair(after(values, belt[-2]) if len(belt) > 1 else values))
        return belt[-1]

    query_own = w_query.transpose(1, 0, 2)
    query_pair = [on_belt(query_own[at : at + 2]) for at in range(0, EA, 2)]
    query_ws = [[query_own], query_pair]

    blocks, scale_one, chunks = pack(
        places, after(tokens, query_own), routes_att, parts, devices
    )
    chunks[1] = after(chunks[1], by_block)
    came = after(swap(chunks), belt[0])
    token_pieces = gather_pieces(came, "tensor")
    dense_pieces = gather_pieces(
        after(jnp.concatenate([w_key, w_value], axis=1), came), "expert", far
    )
    normed_own, normed_pair, routes_far = unpack(
        [after(token_pieces[r], belt[2]) if r == 3 else token_pieces[r] for r in range(parts)],
        by_block[:2, 0].astype(F32),
    )
    normed_far = [normed_own, normed_pair]
    for k in mine:
        dense_pieces[k ^ 1] = on_belt(dense_pieces[k])
    dense_pieces = [dense_pieces[j] for j in range(devices)]
    normed_blocks = (blocks.astype(F32) * scale_one * gain_one).astype(BF16)
    output_own = after(w_output, normed_own).transpose(1, 0, 2)
    output_pair = [on_belt(output_own[at : at + 2]) for at in range(0, EA, 2)]
    output_ws = [[output_own], output_pair]
    routes_one = by_part(after(routes_att, normed_own))

    chosen_one = chosen_of(routes_one, EA)
    gates_one = pair_gates(
        jnp.einsum("jtd,jkd->tk", normed_blocks, route_one, preferred_element_type=F32), chosen_one
    )

    def project_sum(xs, ws):
        early = [k for k in mine if k & 2][::-1]
        middle = [k for k in mine if k and not k & 2]
        found = project(tuple(early), xs, ws, routes_far, BF16)
        chunks = [dict(zip(early, found[choice::2])) for choice in range(2)]
        came = [{k: hop(chunks[c][k], "expert", 2) for k in early} for c in range(2)]
        ready = after(xs[0], came[0][early[0]])
        found = project(tuple(middle), [ready, xs[1]], ws, routes_far, F32)
        sent = []
        for c in range(2):
            held = dict(zip(middle, found[c::2]))
            held = {k: (held[k] + came[c][k + 2].astype(F32)).astype(BF16) for k in middle}
            here = []
            for bit in far[:-1][::-1]:
                for k in sorted(held, reverse=True):
                    if k & bit:
                        sent.append(held.pop(k))
                        arrived = hop(sent[-1], "expert", bit)
                        if k == bit:
                            here.append(arrived)
                        else:
                            held[k ^ bit] = (held[k ^ bit].astype(F32) + arrived.astype(F32)).astype(BF16)
            came[c] = [came[c][2], *here]
        ready = after(xs[0], *sent)
        sums = list(project((0,), [ready, xs[1]], ws, routes_far, F32))
        for c in range(2):
            for one in came[c]:
                sums[c] = sums[c] + one.astype(F32)
        return sums, sent

    raw, started = project_sum(normed_far, query_ws)
    dense_raw = dense_rows(normed_blocks, dense_pieces)
    at_row = (order[:, None] * share + jnp.arange(share)).reshape(-1).astype(jnp.int32)
    at_row = after(at_row, *started)
    segment = by_part(after(segment_ids, *started)[0])
    tables = (*angles(at_row), segment[:, None], segment[None, :], at_row[:, None], at_row[None, :])

    routes_mlp = after(routes_mlp, *started)
    chosen_two = chosen_of(routes_mlp, EXPERTS)
    slot_part, slot = slots_of(chosen_two, quarter)
    slot = by_part(jnp.where(slot_part == part, slot, -1)).T
    routes_two = by_part(routes_mlp).T
    own_chosen = routes_two[:, None, :share] == jnp.arange(EXPERTS, dtype=jnp.int32)[None, :, None]
    own_chosen = own_chosen.astype(F32)
    up = arrange(places, after(cotangent, *started), parts, devices)
    own_up = up[:, :share].astype(F32)
    slots = EXPERTS * quarter

    raw = after(raw, slot, routes_two, own_chosen, up, *tables)
    query, key, lse, mixed, *mixed_sent = attend(raw, dense_raw, gates_one, tables)
    mixed_pieces = gather_far(*mixed_sent)
    branch = to_owners(mixed_pieces, routes_far, output_ws, parts)
    own_tokens = blocks[:, :share]
    hidden, scale_two, own_two = hidden_rows(own_tokens, gain_two, branch)

    rows, dexpert, gates_two = dispatch(
        places, slot, routes_two, route_two, up, gather_pieces(own_two, "tensor"), slots
    )

    def to_experts(values):
        shaped = values.reshape(EXPERTS, 1, quarter, D)
        shaped = jnp.broadcast_to(shaped, (EXPERTS, group, quarter, D)).reshape(devices, quarter, D)
        return lax.all_to_all(shaped, "expert", 0, 0, tiled=True).reshape(devices * quarter, D)

    def back_home(summed):
        summed = summed.astype(BF16).reshape(devices, quarter, D)
        back = lax.all_to_all(summed, "expert", 0, 0, tiled=True)
        back = back.reshape(EXPERTS, group, quarter, D)
        if group > 1:
            back = jnp.sum(back.astype(F32), axis=1).astype(BF16)
        return back.reshape(slots, D)

    turned = (((1,), (1,)), ((), ()))

    def forward(half):
        gate_pre = jnp.dot(half, w_gate[0], preferred_element_type=F32)
        up_pre = jnp.dot(half, w_up[0], preferred_element_type=F32)
        return gate_pre, up_pre, (jax.nn.silu(gate_pre) * up_pre).astype(BF16)

    def backward(half, gate_pre, up_pre):
        dacted = lax.dot_general(half, w_down[0], turned, preferred_element_type=F32)
        sigma = jax.nn.sigmoid(gate_pre)
        dup = (dacted * gate_pre * sigma).astype(BF16)
        dgate = (dacted * up_pre * sigma * (1.0 + gate_pre * (1.0 - sigma))).astype(BF16)
        dinput = lax.dot_general(dgate, w_gate[0], turned, preferred_element_type=F32)
        dinput += lax.dot_general(dup, w_up[0], turned, preferred_element_type=F32)
        return dgate, dup, dinput.astype(BF16)

    assert parts == 4
    came_rows = to_experts(rows)
    far_rows = hop(came_rows, "tensor", 2)
    row_halves = [jnp.concatenate([came_rows, hop(came_rows, "tensor", 1)])]
    pre = [forward(row_halves[0])]
    came_grads = to_experts(after(dexpert, came_rows))
    far_grads = hop(came_grads, "tensor", 2)
    far_rows = after(far_rows, came_grads, pre[0][2])
    row_halves.append(jnp.concatenate([far_rows, hop(far_rows, "tensor", 1)]))
    pre.append(forward(row_halves[1]))
    expert_part = [
        jnp.dot(acted, w_down[0], preferred_element_type=F32).astype(BF16)
        for _, _, acted in pre[::-1]
    ][::-1]

    pair_normed = pair(after(normed_far[1], came_grads))
    pair_routes = pair(after(routes_far, came_grads).astype(BF16).transpose(0, 2, 1))
    far_grads = after(far_grads, *expert_part, pair_normed, pair_routes)
    pair_routes = pair_routes.transpose(0, 2, 1).astype(jnp.int32)
    grad_halves = [
        jnp.concatenate([one, hop(one, "tensor", 1)]) for one in (came_grads, far_grads)
    ]

    def sum_far(half):
        far_chunk, last = jnp.split(half, 2)
        return (far_chunk.astype(F32) + hop(last, "tensor", 1).astype(F32)).astype(BF16)

    def sum_near(half, came):
        chunk, last = jnp.split(half, 2)
        return chunk.astype(F32) + hop(last, "tensor", 1).astype(F32) + came.astype(F32)

    expert_far = sum_far(expert_part[1])
    expert_out = back_home(sum_near(expert_part[0], hop(expert_far, "tensor", 2)))
    back_far = backward(
        after(grad_halves[1], *expert_part), *pre[1][:2]
    )
    input_far = sum_far(back_far[2])
    back_near = backward(
        after(grad_halves[0], input_far), *pre[0][:2]
    )
    input_near = sum_near(back_near[2], hop(input_far, "tensor", 2))
    dreturned = back_home(input_near)

    expert_rows, dout_rows = jnp.concatenate(row_halves), jnp.concatenate(grad_halves)
    acted = jnp.concatenate([one[2] for one in pre])
    dgate = jnp.concatenate([back_near[0], back_far[0]])
    dup = jnp.concatenate([back_near[1], back_far[1]])
    dgate, dup = after((dgate, dup), expert_out)
    grad_gate = jnp.einsum("rd,rf->df", expert_rows, dgate, preferred_element_type=F32)[None]

    *out_chunks, weighted = combine(places, slot, expert_out, parts, devices, gates_two, dexpert)
    weighted, _ = scatter_sum(
        {r: weighted[:, r * share : (r + 1) * share] for r in range(parts)}, "tensor"
    )
    grad_up = jnp.einsum("rd,rf->df", expert_rows, dup, preferred_element_type=F32)[None]
    dreturned = after(dreturned, grad_gate, grad_up)
    back_chunks = combine(places, slot, dreturned, parts, devices)
    own_gates_two = gates_two[:, :share]
    inner = weighted - own_gates_two * jnp.sum(weighted, axis=0, keepdims=True)
    own_dlogits = jnp.sum(inner[:, None, :] * own_chosen, axis=0)
    dnormed = scatter_sum(dict(enumerate(back_chunks)), "tensor")[0] + jnp.einsum(
        "kt,jkd->jtd", own_dlogits, route_two.astype(F32), precision=PRECISE
    )
    pulled = dnormed * gain_two
    inner_mean = jnp.sum(pulled * hidden, axis=(0, 2), keepdims=True) / D
    dhidden = own_up + scale_two * pulled - hidden * (scale_two * scale_two * scale_two * inner_mean)

    moe, _ = scatter_sum(dict(enumerate(after(out_chunks, dhidden))), "tensor")

    sent = dhidden.astype(BF16)
    up_pieces = gather_pieces(swap(
        [jnp.concatenate([sent[k], sent[k ^ 1]], axis=1) for k in mine]
    ), "tensor")
    dhidden_far = assemble([up_pieces[r] for r in range(parts)])
    pull, started = project_sum(dhidden_far, output_ws)
    grad_output, pair_grad = map_grads(
        [[after(dhidden_far[0], *started), dhidden_far[1]]],
        [routes_far],
        [half for k in mine for half in mixed_pieces[k]],
        (F32, BF16),
    )
    pair_grad = pair(pair_grad)
    mixed_out = output_rows(
        places, gather_pieces(after((hidden + moe).astype(BF16), *started), "tensor"), BF16
    )
    def to_features(partial):
        count = partial.shape[0]
        chunks = jnp.take(partial.transpose(1, 0, 2), me ^ jnp.arange(devices), axis=0)[:, None]
        chunks = jnp.broadcast_to(chunks, (devices, parts, count, depth)).reshape(-1, count, depth)
        return jnp.sum(lax.all_to_all(chunks, ("expert", "tensor"), 0, 0, tiled=True), axis=0)

    part_gain_two = jnp.sum(dnormed * hidden * scale_two, axis=1)[None]
    part_route_two = jnp.einsum(
        "kt,jtd->kjd", own_dlogits, own_two.astype(F32), precision=PRECISE
    )

    pull = after(pull, grad_output)
    *dqueries, ddense, dgates_one = attend_back(query, key, lse, mixed, pull, gates_one, tables)
    dquery_pieces = gather_far(*dqueries)
    acted = after(acted, dquery_pieces[2][0])
    grad_down = jnp.einsum("rf,rd->fd", acted, dout_rows, preferred_element_type=F32)[None]
    pair_dquery = {k: [pair(one) for one in dquery_pieces[k]] for k in mine}
    dense_far = gather_pieces(ddense, "expert", far)
    dense_back = dense_rows_back(ddense, dense_pieces, parts)
    dense_share, _ = scatter_sum({r: dense_back[r] for r in range(parts)}, "tensor")
    dnormed_came = to_owners(
        dquery_pieces,
        routes_far,
        query_ws,
        parts,
        ((*pair_dquery[0], grad_down), pair_dquery[2], pair_dquery[4]),
    )
    dgates_one, _ = scatter_sum(
        {r: dgates_one[r * share : (r + 1) * share] for r in range(parts)}, "tensor"
    )
    grad_dense, pair_grad_dense = dense_grad(
        normed_far, [dense_far[k] for k in mine], (F32, BF16)
    )
    grad_dense = grad_dense + pair(pair_grad_dense).astype(F32)
    (grad_query,) = map_grads(
        [[normed_far[0]], [after(pair_normed, *dnormed_came.values())]],
        [routes_far, pair_routes],
        [half for side in (dquery_pieces, pair_dquery) for k in mine for half in side[k]],
        (F32,),
    )
    grad_key, grad_value = grad_dense[:, :width], grad_dense[:, width:]

    own_gates, own_scale = gates_one[:share], scale_one[:share]
    own_dlogits_one = logit_grad(own_gates, own_gates * dgates_one, chosen_one[:share])
    dnormed_came[0] = after(dnormed_came[0], *pair_dquery[6], dense_far[4])
    whole = jnp.stack(
        [
            dnormed_came[k][:, b * depth : (b + 1) * depth].astype(F32)
            for k in mine
            for b in range(2)
        ]
    )
    dnormed_one = whole + dense_share + jnp.einsum(
        "tk,jkd->jtd", own_dlogits_one, route_one.astype(F32), precision=PRECISE
    )
    pulled_one = dnormed_one * gain_one
    token_rows = own_tokens.astype(F32)
    inner_one = jnp.sum(pulled_one * token_rows, axis=(0, 2), keepdims=True) / D
    own_grad = (
        dhidden
        + own_scale * pulled_one
        - token_rows * (own_scale * own_scale * own_scale * inner_one)
    )
    own_grad = after(own_grad.astype(BF16), dense_far[6])
    grad_pieces = gather_pieces(own_grad, "tensor")
    grad_tokens = output_rows(places, {**grad_pieces, 3: after(grad_pieces[3], grad_dense)}, F32)
    part_gain_one = jnp.sum(dnormed_one * token_rows * own_scale, axis=1)[None]
    part_route_one = jnp.einsum(
        "tk,jtd->kjd", own_dlogits_one, normed_blocks[:, :share].astype(F32), precision=PRECISE
    )

    smalls = to_features(
        jnp.concatenate([part_gain_two, part_route_two, part_gain_one, part_route_one])
    )
    small_two, small_one = smalls[:9], smalls[9:]
    return (
        mixed_out,
        grad_tokens,
        small_one[0],
        small_one[1:].T,
        grad_query,
        grad_key,
        grad_value,
        grad_output + pair_grad.astype(F32),
        small_two[0],
        small_two[1:].T,
        grad_gate,
        grad_up,
        grad_down,
    )


def solution(mesh):
    in_specs = (
        P("expert", None),
        P("expert", None),
        P("expert", None),
        P("expert", None),
        P("expert", None),
        P("expert"),
        P("expert", None),
        P("expert", None, "tensor"),
        P("expert", "tensor"),
        P("expert", "tensor"),
        P("expert", None, "tensor"),
        P("expert"),
        P("expert", None),
        P("expert", None, "tensor"),
        P("expert", None, "tensor"),
        P("expert", "tensor", None),
    )
    out_specs = (
        P("expert", None),
        P("expert", None),
        P("expert"),
        P("expert", None),
        P("expert", None, "tensor"),
        P("expert", "tensor"),
        P("expert", "tensor"),
        P("expert", None, "tensor"),
        P("expert"),
        P("expert", None),
        P("expert", None, "tensor"),
        P("expert", None, "tensor"),
        P("expert", "tensor", None),
    )
    return jax.shard_map(body, mesh=mesh, in_specs=in_specs, out_specs=out_specs, check_vma=False)
```

```python
import functools

import jax
import jax.numpy as jnp
from jax import lax
from jax.experimental import pallas as pl
from jax.experimental.pallas import tpu as pltpu
from jax.sharding import PartitionSpec as P

D = 2048
HEAD_DIM = 128
EA = 8
EXPERTS = 8
CAP = 96
EPSILON = 1e-05
ROTARY_BASE = 10000.0
VMEM = 56 * 1024 * 1024
F32 = jnp.float32
BF16 = jnp.bfloat16
PRECISE = lax.Precision.HIGHEST


def hop(values, axis, bit):
    size = lax.axis_size(axis)
    return lax.ppermute(values, axis, [(i, i ^ bit) for i in range(size)])


def bits_of(axis):
    size, bits = lax.axis_size(axis), []
    while 1 << len(bits) < size:
        bits.append(1 << len(bits))
    return bits[::-1]


def gather_pieces(values, axis, bits=None):
    pieces = {0: values}
    for bit in bits_of(axis) if bits is None else bits:
        for known in sorted(pieces):
            pieces[known | bit] = hop(pieces[known], axis, bit)
    return pieces


def scatter_sum(chunks, axis, bits=None, sent_as=None):
    held, came = dict(chunks), []
    for bit in (bits_of(axis) if bits is None else bits)[::-1]:
        for k in sorted(held, reverse=True):
            if k & bit:
                sent = held.pop(k)
                came.append(hop(sent.astype(sent_as or sent.dtype), axis, bit))
                held[k ^ bit] = held[k ^ bit].astype(F32) + came[-1].astype(F32)
                if k ^ bit:
                    held[k ^ bit] = held[k ^ bit].astype(sent_as or sent.dtype)
    return held[0], came


def after(values, *earlier):
    return lax.optimization_barrier((values, *earlier))[0]


def whole_spec(shape):
    zeros = (0,) * len(shape)
    return pl.BlockSpec(shape, lambda *_: zeros)


def params(*arrays):
    held = 3 * sum(one.size * one.dtype.itemsize for one in arrays) + (12 << 20)
    return pltpu.CompilerParams(vmem_limit_bytes=min(VMEM, held) if arrays else 16 << 20)


def one_of(routes, kind):
    return (routes == kind).astype(F32).astype(BF16)


def map_of(refs, kind):
    each = EA // len(refs)
    return refs[kind // each][kind % each]


def project_kernel(which, counts, *refs):
    x_refs, refs = refs[: len(counts)], refs[len(counts) :]
    w_refs = []
    for count in counts:
        w_refs.append(refs[:count])
        refs = refs[count:]
    routes_ref, outs = refs[0], refs[1:]
    for at, k in enumerate(which):
        routes = routes_ref[k // 2]
        for choice in range(2):
            total = jnp.zeros(outs[0].shape, F32)
            for x_ref, maps in zip(x_refs, w_refs):
                x = x_ref[k // 2]
                each = EA // len(maps)
                for first, w_ref in zip(range(0, EA, each), maps):
                    spread = jnp.concatenate(
                        [
                            x * one_of(routes[:, choice : choice + 1], kind)
                            for kind in range(first, first + each)
                        ],
                        axis=1,
                    )
                    flat = w_ref[...].reshape(each * x.shape[1], w_ref.shape[2])
                    total += jnp.dot(spread, flat, preferred_element_type=F32)
            outs[2 * at + choice][...] = total.astype(outs[0].dtype)


def project(which, xs, ws, routes, dtype):
    _, length, depth = xs[0].shape
    width = ws[0][0].shape[2]
    outs = [jax.ShapeDtypeStruct((length, width), dtype)] * (2 * len(which))
    maps = [one for side in ws for one in side]
    return pl.pallas_call(
        functools.partial(project_kernel, which, [len(side) for side in ws]),
        out_shape=outs,
        compiler_params=params(*xs, *maps, *outs),
        cost_estimate=pl.CostEstimate(flops=0, bytes_accessed=0, transcendentals=0),
    )(*xs, *maps, routes)


def contract_kernel(which, counts, parts, routes_ref, *refs):
    w_refs = []
    for count in counts:
        w_refs.append(refs[:count])
        refs = refs[count:]
    rows, outs = refs[: 2 * len(which)], refs[2 * len(which) :]
    share, depth = outs[0].shape[1], w_refs[0][0].shape[1]
    turned = (((1,), (1,)), ((), ()))
    for at, k in enumerate(which):
        routes = routes_ref[k // 2]
        first, second = rows[2 * at][...], rows[2 * at + 1][...]
        totals = [jnp.zeros((share * parts, depth), F32)] * len(counts)
        for kind in range(EA):
            ones = one_of(routes, kind)
            picked = first * ones[:, 0:1] + second * ones[:, 1:2]
            totals = [
                total
                + lax.dot_general(picked, map_of(maps, kind), turned, preferred_element_type=F32)
                for total, maps in zip(totals, w_refs)
            ]
        for b, total in enumerate(totals):
            for r in range(parts):
                outs[r][at, :, b * depth : (b + 1) * depth] = total[
                    r * share : (r + 1) * share
                ].astype(outs[r].dtype)


def contract(which, pieces, routes, ws, parts):
    rows = [half for k in which for half in pieces[k]]
    _, length, _ = routes.shape
    depth, width = ws[0][0].shape[1:]
    shape = (len(which), length // parts, depth * len(ws))
    maps = [one for side in ws for one in side]
    return pl.pallas_call(
        functools.partial(contract_kernel, which, [len(side) for side in ws], parts),
        out_shape=[
            jax.ShapeDtypeStruct(shape, BF16 if r % 2 else F32) for r in range(parts)
        ],
        compiler_params=params(*maps, *rows),
        cost_estimate=pl.CostEstimate(flops=0, bytes_accessed=0, transcendentals=0),
    )(routes, *maps, *rows)


def to_owners(pieces, routes, ws, parts, ties=((), (), ())):
    came, order, last = {}, sorted(pieces), ()
    for at_call, which in enumerate((order[:-1], order[-1:])):
        tied = after(routes, *ties[at_call], *last)
        last = contract(tuple(which), pieces, tied, ws, parts)
        summed, _ = scatter_sum(dict(enumerate(last)), "tensor", None, BF16)
        if at_call:
            summed = after(summed, *ties[2])
        for at, k in enumerate(which):
            came[k] = hop(summed[at].astype(BF16), "expert", k) if k else summed[at]
    return came


def arrange_kernel(parts, places, x_ref, out_ref):
    count, length, depth = out_ref.shape
    share = length // parts
    for r in range(parts):
        spot = pl.ds(pl.multiple_of((places[1] ^ r) * share, share), share)
        for j in range(count):
            out_ref[places[0] ^ j, r * share : (r + 1) * share, :] = x_ref[
                spot, j * depth : (j + 1) * depth
            ]


def arrange(places, x, parts, count):
    shape = (count, x.shape[0], x.shape[1] // count)
    return pl.pallas_call(
        functools.partial(arrange_kernel, parts),
        out_shape=jax.ShapeDtypeStruct(shape, BF16),
        grid_spec=pltpu.PrefetchScalarGridSpec(
            num_scalar_prefetch=1,
            grid=(1,),
            in_specs=[whole_spec(x.shape)],
            out_specs=whole_spec(shape),
        ),
        compiler_params=params(x),
        cost_estimate=pl.CostEstimate(flops=0, bytes_accessed=0, transcendentals=0),
    )(places, x)


def pack_kernel(parts, places, x_ref, routes_ref, blocks_ref, scale_ref, *outs):
    count, length, depth = blocks_ref.shape
    share = length // parts
    for r in range(parts):
        spot = pl.ds(pl.multiple_of((places[1] ^ r) * share, share), share)
        rows = slice(r * share, (r + 1) * share)
        squares = jnp.zeros((share, 1), F32)
        for j in range(count):
            block = x_ref[spot, j * depth : (j + 1) * depth]
            blocks_ref[places[0] ^ j, rows, :] = block
            wide = block.astype(F32)
            squares += jnp.sum(wide * wide, axis=1, keepdims=True)
        scale = lax.rsqrt(squares / D + EPSILON)
        scale_ref[rows, :] = scale
        if r == 0:
            high = scale.astype(BF16).astype(F32)
            middle = (scale - high).astype(BF16).astype(F32)
            routes = routes_ref[spot, :].astype(F32)
            columns = [routes[:, 0:1], routes[:, 1:2], high, middle, scale - high - middle]
            lane = lax.broadcasted_iota(jnp.int32, (share, 128), 1)
            extra = jnp.zeros((share, 128), F32)
            for at, column in enumerate(columns):
                extra = jnp.where(lane == at, column, extra)
    for at, out_ref in enumerate(outs):
        for b in range(2):
            out_ref[:, b * depth : (b + 1) * depth] = blocks_ref[2 * at + b, :share, :]
        out_ref[:, 2 * depth :] = extra.astype(BF16)


def pack(places, x, routes, parts, count):
    length, depth = x.shape[0], x.shape[1] // count
    shapes = [(count, length, depth), (length, 1)]
    shapes += [(length // parts, 2 * depth + 128)] * (count // 2)
    types = [BF16, F32] + [BF16] * (count // 2)
    blocks, scale, *chunks = pl.pallas_call(
        functools.partial(pack_kernel, parts),
        out_shape=[jax.ShapeDtypeStruct(*one) for one in zip(shapes, types)],
        grid_spec=pltpu.PrefetchScalarGridSpec(
            num_scalar_prefetch=1,
            grid=(1,),
            in_specs=[whole_spec(x.shape), whole_spec(routes.shape)],
            out_specs=[whole_spec(one) for one in shapes],
        ),
        compiler_params=params(x),
        cost_estimate=pl.CostEstimate(flops=0, bytes_accessed=0, transcendentals=0),
    )(places, x, routes)
    return blocks, scale, chunks


def unpack_kernel(parts, *refs):
    pieces, (gain_ref, *outs, routes_ref) = refs[:parts], refs[parts:]
    share, depth = pieces[0].shape[1], outs[0].shape[2]
    for r, piece in enumerate(pieces):
        rows = slice(r * share, (r + 1) * share)
        for k in range(piece.shape[0]):
            extra = piece[k, :, 2 * depth :].astype(F32)
            scale = extra[:, 2:3] + extra[:, 3:4] + extra[:, 4:5]
            routes_ref[k, rows, :] = extra[:, 0:2].astype(jnp.int32)
            for b, out_ref in enumerate(outs):
                values = piece[k, :, b * depth : (b + 1) * depth].astype(F32)
                out_ref[k, rows, :] = (values * scale * gain_ref[b : b + 1, :]).astype(BF16)


def unpack(pieces, gains):
    count, share, _ = pieces[0].shape
    shape = (count, share * len(pieces), gains.shape[1])
    return pl.pallas_call(
        functools.partial(unpack_kernel, len(pieces)),
        out_shape=[
            *[jax.ShapeDtypeStruct(shape, BF16)] * 2,
            jax.ShapeDtypeStruct((*shape[:2], 2), jnp.int32),
        ],
        compiler_params=params(*pieces, *pieces),
        cost_estimate=pl.CostEstimate(flops=0, bytes_accessed=0, transcendentals=0),
    )(*pieces, gains)


def assemble_kernel(parts, *refs):
    pieces, outs = refs[:parts], refs[parts:]
    _, share, both = pieces[0].shape
    depth = both // 2
    for r, piece in enumerate(pieces):
        for b, out_ref in enumerate(outs):
            out_ref[:, r * share : (r + 1) * share, :] = piece[:, :, b * depth : (b + 1) * depth]


def assemble(pieces):
    count, share, both = pieces[0].shape
    shape = (count, share * len(pieces), both // 2)
    return pl.pallas_call(
        functools.partial(assemble_kernel, len(pieces)),
        out_shape=[jax.ShapeDtypeStruct(shape, BF16)] * 2,
        compiler_params=params(*pieces, *pieces),
        cost_estimate=pl.CostEstimate(flops=0, bytes_accessed=0, transcendentals=0),
    )(*pieces)


def output_kernel(parts, places, *refs):
    pieces, out_ref = refs[:parts], refs[-1]
    count, share, depth = pieces[0].shape
    for r, piece in enumerate(pieces):
        spot = pl.ds(pl.multiple_of((places[1] ^ r) * share, share), share)
        for j in range(count):
            out_ref[spot, j * depth : (j + 1) * depth] = piece[places[0] ^ j].astype(out_ref.dtype)


def output_rows(places, pieces, dtype):
    pieces = [pieces[r] for r in sorted(pieces)]
    count, share, depth = pieces[0].shape
    shape = (share * len(pieces), count * depth)
    return pl.pallas_call(
        functools.partial(output_kernel, len(pieces)),
        out_shape=jax.ShapeDtypeStruct(shape, dtype),
        grid_spec=pltpu.PrefetchScalarGridSpec(
            num_scalar_prefetch=1,
            grid=(1,),
            in_specs=[whole_spec(one.shape) for one in pieces],
            out_specs=whole_spec(shape),
        ),
        compiler_params=params(*pieces, *pieces),
        cost_estimate=pl.CostEstimate(flops=0, bytes_accessed=0, transcendentals=0),
    )(places, *pieces)


def hidden_kernel(own_ref, gain_ref, *refs):
    came, (hidden_ref, scale_ref, normed_ref) = refs[:-3], refs[-3:]
    depth = own_ref.shape[2]
    squares = 0.0
    for at, one in enumerate(came):
        for b in range(2):
            hidden = own_ref[2 * at + b].astype(F32) + one[:, b * depth : (b + 1) * depth].astype(F32)
            hidden_ref[2 * at + b] = hidden
            squares += jnp.sum(hidden * hidden, axis=1, keepdims=True)
    scale = lax.rsqrt(squares / D + EPSILON)
    scale_ref[...] = scale
    for j in range(2 * len(came)):
        normed_ref[j] = (hidden_ref[j] * scale * gain_ref[j]).astype(BF16)


def hidden_rows(own, gain, came):
    came = [came[k] for k in sorted(came)]
    count, share, depth = own.shape
    return pl.pallas_call(
        hidden_kernel,
        out_shape=[
            jax.ShapeDtypeStruct(own.shape, F32),
            jax.ShapeDtypeStruct((share, 1), F32),
            jax.ShapeDtypeStruct(own.shape, BF16),
        ],
        compiler_params=params(own, own, own, own),
        cost_estimate=pl.CostEstimate(flops=0, bytes_accessed=0, transcendentals=0),
    )(own, gain, *came)


def dispatch_kernel(parts, places, slot_ref, routes_ref, router_ref, up_ref, *refs):
    pieces, (rows_ref, grads_ref, gates_ref) = refs[:parts], refs[parts:]
    count, _, depth = pieces[0].shape
    slots, length = rows_ref.shape[0], slot_ref.shape[1]
    logits = jnp.zeros((EXPERTS, length), F32)
    for j in range(count):
        block = jnp.concatenate([piece[j] for piece in pieces])
        logits += lax.dot_general(
            router_ref[j], block, (((1,), (1,)), ((), ())), preferred_element_type=F32
        )
    kinds = lax.broadcasted_iota(jnp.int32, (EXPERTS, length), 0)
    picked = [
        jnp.sum(jnp.where(kinds == routes_ref[c : c + 1, :], logits, 0.0), axis=0, keepdims=True)
        for c in range(2)
    ]
    top = jnp.maximum(picked[0], picked[1])
    powers = [jnp.exp(one - top) for one in picked]
    gates = [one / (powers[0] + powers[1]) for one in powers]
    slot_at = lax.broadcasted_iota(jnp.int32, (slots, length), 0)
    here = [slot_at == slot_ref[c : c + 1, :] for c in range(2)]
    gate = jnp.where(here[0], gates[0], jnp.where(here[1], gates[1], 0.0))
    gate = jnp.sum(gate, axis=1, keepdims=True)
    place = jnp.where(here[0] | here[1], 1.0, 0.0).astype(BF16)
    for j in range(count):
        lanes = slice(j * depth, (j + 1) * depth)
        block = jnp.concatenate([piece[places[0] ^ j] for piece in pieces])
        rows_ref[:, lanes] = jnp.dot(place, block, preferred_element_type=F32).astype(BF16)
        grads = jnp.dot(place, up_ref[places[0] ^ j], preferred_element_type=F32)
        grads_ref[:, lanes] = (grads * gate).astype(BF16)
    for c in range(2):
        gates_ref[c : c + 1, :] = gates[c]


def dispatch(places, slot, routes, router, up, pieces, slots):
    pieces = [pieces[r] for r in sorted(pieces)]
    operands = (slot, routes, router, up, *pieces)
    shapes = [(slots, D), (slots, D), slot.shape]
    return pl.pallas_call(
        functools.partial(dispatch_kernel, len(pieces)),
        out_shape=[
            jax.ShapeDtypeStruct(shape, dtype) for shape, dtype in zip(shapes, (BF16, BF16, F32))
        ],
        grid_spec=pltpu.PrefetchScalarGridSpec(
            num_scalar_prefetch=1,
            grid=(1,),
            in_specs=[whole_spec(one.shape) for one in operands],
            out_specs=[whole_spec(shape) for shape in shapes],
        ),
        compiler_params=params(up, up, *pieces),
        cost_estimate=pl.CostEstimate(flops=0, bytes_accessed=0, transcendentals=0),
    )(places, *operands)


def combine_kernel(parts, weigh, places, slot_ref, values_ref, *refs):
    extra, outs = refs[: 2 * weigh], refs[2 * weigh :]
    count, share, depth = outs[0].shape
    slots, length = values_ref.shape[0], slot_ref.shape[1]
    slot_at = lax.broadcasted_iota(jnp.int32, (slots, length), 0)
    here = [slot_at == slot_ref[c : c + 1, :] for c in range(2)]
    if weigh:
        gates_ref, grads_ref = extra
        place = jnp.where(
            here[0], gates_ref[0:1, :], jnp.where(here[1], gates_ref[1:2, :], 0.0)
        ).astype(BF16)
        weighted = jnp.sum(
            values_ref[...].astype(F32) * grads_ref[...].astype(F32), axis=1, keepdims=True
        )
        for c in range(2):
            outs[-1][c : c + 1, :] = jnp.sum(
                jnp.where(here[c], weighted, 0.0), axis=0, keepdims=True
            )
    else:
        place = jnp.where(here[0] | here[1], 1.0, 0.0).astype(BF16)
    over_slots = (((0,), (0,)), ((), ()))
    for j in range(count):
        total = lax.dot_general(
            place, values_ref[:, j * depth : (j + 1) * depth], over_slots, preferred_element_type=F32
        ).astype(BF16)
        for r in range(parts):
            outs[r][places[0] ^ j] = total[r * share : (r + 1) * share]


def combine(places, slot, values, parts, count, *extra):
    slots, length = values.shape[0], slot.shape[1]
    shape = (count, length // parts, D // count)
    outs = [jax.ShapeDtypeStruct(shape, BF16)] * parts
    outs += [jax.ShapeDtypeStruct((2, length), F32)] * bool(extra)
    operands = (slot, values, *extra)
    return pl.pallas_call(
        functools.partial(combine_kernel, parts, 1 if extra else 0),
        out_shape=outs,
        grid_spec=pltpu.PrefetchScalarGridSpec(
            num_scalar_prefetch=1,
            grid=(1,),
            in_specs=[whole_spec(one.shape) for one in operands],
            out_specs=[whole_spec(one.shape) for one in outs],
        ),
        compiler_params=params(values, *extra, *outs),
        cost_estimate=pl.CostEstimate(flops=0, bytes_accessed=0, transcendentals=0),
    )(places, *operands)


def map_grads_kernel(n_x, n_sides, *refs):
    x_refs, routes_refs = refs[:n_x], refs[n_x : n_x + n_sides]
    outs, (turned, picked) = refs[-2 - n_x // n_sides : -2], refs[-2:]
    rows = refs[n_x + n_sides : -2 - n_x // n_sides]
    count, length, depth = x_refs[0].shape
    blocks = n_x // n_sides
    for at, x_ref in enumerate(x_refs):
        side, block = at // blocks, at % blocks
        for k in range(count):
            here = slice((side * count + k) * length, (side * count + k + 1) * length)
            turned[block * depth : (block + 1) * depth, here] = x_ref[k].T
    for kind in range(EA):
        for side, routes_ref in enumerate(routes_refs):
            for k in range(count):
                ones = one_of(routes_ref[k], kind)
                at = side * count + k
                picked[at * length : (at + 1) * length, :] = (
                    rows[2 * at][...] * ones[:, 0:1] + rows[2 * at + 1][...] * ones[:, 1:2]
                )
        for block, out_ref in enumerate(outs):
            out_ref[:, kind, :] = jnp.dot(
                turned[block * depth : (block + 1) * depth, :],
                picked[...],
                preferred_element_type=F32,
            ).astype(out_ref.dtype)


def map_grads(sides, routes, rows, dtypes):
    xs = [x for side in sides for x in side]
    count, length, depth = xs[0].shape
    width = rows[0].shape[1]
    total = len(sides) * count * length
    return pl.pallas_call(
        functools.partial(map_grads_kernel, len(xs), len(sides)),
        out_shape=[jax.ShapeDtypeStruct((depth, EA, width), dtype) for dtype in dtypes],
        scratch_shapes=[
            pltpu.VMEM((depth * len(dtypes), total), BF16),
            pltpu.VMEM((total, width), BF16),
        ],
        compiler_params=pltpu.CompilerParams(vmem_limit_bytes=VMEM),
        cost_estimate=pl.CostEstimate(flops=0, bytes_accessed=0, transcendentals=0),
    )(*xs, *routes, *rows)


def turn(values, cosine, sine):
    return values * cosine + pltpu.roll(values, HEAD_DIM // 2, 1) * sine


def rows_kernel(x_ref, *refs):
    pieces, out_ref = refs[:-1], refs[-1]
    total = jnp.zeros(out_ref.shape, F32)
    for j, piece in enumerate(pieces):
        total += jnp.dot(x_ref[j], piece[...], preferred_element_type=F32)
    out_ref[...] = total


def dense_rows(x, pieces):
    _, length, depth = x.shape
    width = pieces[0].shape[1]
    return pl.pallas_call(
        rows_kernel,
        out_shape=jax.ShapeDtypeStruct((length, width), F32),
        compiler_params=params(x, *pieces),
        cost_estimate=pl.CostEstimate(flops=0, bytes_accessed=0, transcendentals=0),
    )(x, *pieces)


def rows_back_kernel(drows_ref, *refs):
    pieces, out_ref = refs[:-1], refs[-1]
    parts, share = out_ref.shape[0], out_ref.shape[2]
    for j, piece in enumerate(pieces):
        total = lax.dot_general(
            drows_ref[...], piece[...], (((1,), (1,)), ((), ())), preferred_element_type=F32
        ).astype(BF16)
        for r in range(parts):
            out_ref[r, j] = total[r * share : (r + 1) * share]


def dense_rows_back(drows, pieces, parts):
    length, width = drows.shape
    depth = pieces[0].shape[0]
    shape = (parts, len(pieces), length // parts, depth)
    return pl.pallas_call(
        rows_back_kernel,
        out_shape=jax.ShapeDtypeStruct(shape, BF16),
        compiler_params=params(drows, *pieces),
        cost_estimate=pl.CostEstimate(flops=0, bytes_accessed=0, transcendentals=0),
    )(drows, *pieces)


def dense_grad_kernel(n_x, *refs):
    x_refs, outs = refs[:n_x], refs[-n_x:]
    rows = refs[n_x:-n_x]
    for x_ref, out_ref in zip(x_refs, outs):
        total = jnp.zeros(out_ref.shape, F32)
        for at, one in enumerate(rows):
            total += jnp.dot(x_ref[at].T, one[...], preferred_element_type=F32)
        out_ref[...] = total.astype(out_ref.dtype)


def dense_grad(xs, rows, dtypes):
    depth, width = xs[0].shape[2], rows[0].shape[1]
    return pl.pallas_call(
        functools.partial(dense_grad_kernel, len(xs)),
        out_shape=[jax.ShapeDtypeStruct((depth, width), dtype) for dtype in dtypes],
        compiler_params=params(*xs, *rows),
        cost_estimate=pl.CostEstimate(flops=0, bytes_accessed=0, transcendentals=0),
    )(*xs, *rows)


def allowed_of(seg_col, seg_row, place_col, place_row):
    return (seg_col[...] == seg_row[...]) & (place_row[...] <= place_col[...])


def attend_kernel(
    first_ref, second_ref, dense_ref, gates_ref, cos_ref, sin_ref, seg_col, seg_row, place_col, place_row, query_ref, key_ref, lse_ref, mixed_ref, *send_refs
):
    width = first_ref.shape[1]
    heads = width // HEAD_DIM
    cosine, sine = cos_ref[...], sin_ref[...]
    allowed = allowed_of(seg_col, seg_row, place_col, place_row)
    for head in range(heads):
        at = head * HEAD_DIM
        key_at, value_at = slice(at, at + HEAD_DIM), slice(width + at, width + at + HEAD_DIM)
        key = turn(dense_ref[:, key_at], cosine, sine).astype(BF16)
        value = dense_ref[:, value_at].astype(BF16)
        key_ref[:, key_at] = key
        key_ref[:, value_at] = value
        for choice, raw_ref in enumerate((first_ref, second_ref)):
            here = slice(choice * width + at, choice * width + at + HEAD_DIM)
            query = turn(raw_ref[:, key_at], cosine, sine).astype(BF16)
            query_ref[:, here] = query
            scores = lax.dot_general(
                query, key, (((1,), (1,)), ((), ())), preferred_element_type=F32
            ) * HEAD_DIM ** (-0.5)
            scores = jnp.where(allowed, scores, -1e30)
            top = jnp.max(scores, axis=1, keepdims=True)
            lse = top + jnp.log(jnp.sum(jnp.exp(scores - top), axis=1, keepdims=True))
            lse_ref[:, choice * heads + head : choice * heads + head + 1] = lse
            probs = jnp.exp(scores - lse).astype(BF16)
            mixed = jnp.dot(probs, value, preferred_element_type=F32).astype(BF16)
            mixed_ref[:, here] = mixed
            send_refs[choice][:, key_at] = (
                mixed.astype(F32) * gates_ref[:, choice : choice + 1]
            ).astype(BF16)


def attend(raw, dense, gates, tables):
    length, width = raw[0].shape
    return pl.pallas_call(
        attend_kernel,
        out_shape=[
            jax.ShapeDtypeStruct((length, 2 * width), BF16),
            jax.ShapeDtypeStruct((length, 2 * width), BF16),
            jax.ShapeDtypeStruct((length, 2 * width // HEAD_DIM), F32),
            jax.ShapeDtypeStruct((length, 2 * width), BF16),
            *[jax.ShapeDtypeStruct((length, width), BF16)] * 2,
        ],
        compiler_params=pltpu.CompilerParams(vmem_limit_bytes=24 << 20),
        cost_estimate=pl.CostEstimate(flops=0, bytes_accessed=0, transcendentals=0),
    )(*raw, dense, gates, *tables)


def attend_back_kernel(
    query_ref, key_ref, lse_ref, mixed_ref, first_ref, second_ref, gates_ref, cos_ref, sin_ref, seg_col, seg_row, place_col, place_row, *refs
):
    dquery_refs, (dkey_ref, dgates_ref) = refs[:2], refs[2:]
    length = query_ref.shape[0]
    width = query_ref.shape[1] // 2
    heads = width // HEAD_DIM
    cosine, sine = cos_ref[...], sin_ref[...]
    allowed = allowed_of(seg_col, seg_row, place_col, place_row)
    turned = (((1,), (1,)), ((), ()))
    dgates = [jnp.zeros((length, 1), F32), jnp.zeros((length, 1), F32)]
    for head in range(heads):
        at = head * HEAD_DIM
        key_at, value_at = slice(at, at + HEAD_DIM), slice(width + at, width + at + HEAD_DIM)
        key, value = key_ref[:, key_at], key_ref[:, value_at]
        dkey = jnp.zeros((length, HEAD_DIM), F32)
        dvalue = jnp.zeros((length, HEAD_DIM), F32)
        for choice, pull_ref in enumerate((first_ref, second_ref)):
            here = slice(choice * width + at, choice * width + at + HEAD_DIM)
            query, pull = query_ref[:, here], pull_ref[:, key_at]
            dgates[choice] += jnp.sum(mixed_ref[:, here].astype(F32) * pull, axis=1, keepdims=True)
            dmixed = (pull * gates_ref[:, choice : choice + 1]).astype(BF16)
            scores = lax.dot_general(query, key, turned, preferred_element_type=F32) * HEAD_DIM ** (-0.5)
            scores = jnp.where(allowed, scores, -1e30)
            probs = jnp.exp(scores - lse_ref[:, choice * heads + head : choice * heads + head + 1])
            dprobs = lax.dot_general(dmixed, value, turned, preferred_element_type=F32)
            inner = jnp.sum(probs * dprobs, axis=1, keepdims=True)
            dscores = (probs * (dprobs - inner)).astype(BF16)
            dquery = jnp.dot(dscores, key, preferred_element_type=F32) * HEAD_DIM ** (-0.5)
            dquery_refs[choice][:, key_at] = turn(dquery, cosine, -sine).astype(BF16)
            dkey += jnp.dot(dscores.T, query, preferred_element_type=F32)
            dvalue += jnp.dot(probs.astype(BF16).T, dmixed, preferred_element_type=F32)
        dkey_ref[:, key_at] = turn(dkey * HEAD_DIM ** (-0.5), cosine, -sine).astype(BF16)
        dkey_ref[:, value_at] = dvalue.astype(BF16)
    for choice in range(2):
        dgates_ref[:, choice : choice + 1] = dgates[choice]


def attend_back(query, key, lse, mixed, pull, gates, tables):
    length, width = pull[0].shape
    return pl.pallas_call(
        attend_back_kernel,
        out_shape=[
            *[jax.ShapeDtypeStruct((length, width), BF16)] * 2,
            jax.ShapeDtypeStruct(key.shape, BF16),
            jax.ShapeDtypeStruct(gates.shape, F32),
        ],
        compiler_params=pltpu.CompilerParams(vmem_limit_bytes=24 << 20),
        cost_estimate=pl.CostEstimate(flops=0, bytes_accessed=0, transcendentals=0),
    )(query, key, lse, mixed, *pull, gates, *tables)


def angles(places):
    half = HEAD_DIM // 2
    freqs = ROTARY_BASE ** (-(jnp.arange(half, dtype=F32) * 2.0 / HEAD_DIM))
    phase = places.astype(F32)[:, None] * freqs[None, :]
    cosine, sine = jnp.cos(phase), jnp.sin(phase)
    return jnp.concatenate([cosine, cosine], axis=1), jnp.concatenate([-sine, sine], axis=1)


def chosen_of(routes, kinds):
    return (routes[:, :, None] == jnp.arange(kinds, dtype=jnp.int32)).astype(F32)


def pair_gates(logits, chosen):
    return jax.nn.softmax(jnp.sum(logits[:, None, :] * chosen, axis=2), axis=-1)


def logit_grad(gates, weighted, chosen):
    inner = weighted - gates * jnp.sum(weighted, axis=1, keepdims=True)
    return jnp.sum(inner[:, :, None] * chosen, axis=1)


def slots_of(chosen, quarter):
    named = jnp.sum(chosen, axis=1)
    rows = named.shape[0]
    before = (jnp.arange(rows)[:, None] > jnp.arange(rows)[None, :]).astype(F32)
    rank = jnp.sum((before @ named)[:, None, :] * chosen, axis=2).astype(jnp.int32)
    kind = jnp.sum(chosen * jnp.arange(chosen.shape[2], dtype=F32), axis=2).astype(jnp.int32)
    return rank // quarter, kind * quarter + rank % quarter


def body(
    tokens,
    cotangent,
    segment_ids,
    routes_att,
    routes_mlp,
    gain_att,
    router_att,
    w_query,
    w_key,
    w_value,
    w_output,
    gain_mlp,
    router_mlp,
    w_gate,
    w_up,
    w_down,
):
    parts = lax.axis_size("tensor")
    devices = lax.axis_size("expert")
    group = devices // EXPERTS
    length = tokens.shape[0]
    share = length // parts
    quarter = CAP // parts
    depth = gain_att.shape[0]
    width = w_key.shape[1]
    me = lax.axis_index("expert")
    part = lax.axis_index("tensor")
    places = jnp.stack([me, part]).astype(jnp.int32)
    order = part ^ jnp.arange(parts)
    far = bits_of("expert")[:-1]
    mine = range(0, devices, 2)

    def by_part(values):
        shaped = values.reshape(parts, share, *values.shape[1:])
        return jnp.take(shaped, order, axis=0).reshape(values.shape)

    def gather_far(first, second):
        halves = [gather_pieces(one, "expert", far) for one in (first, second)]
        return {k: (halves[0][k], halves[1][k]) for k in mine}

    def pair(values):
        return hop(values, "expert", 1)

    query_own = w_query.transpose(1, 0, 2)
    own_meta = jnp.concatenate(
        [gain_att, gain_mlp, router_att.T.reshape(-1), router_mlp.T.reshape(-1)]
    ).reshape(18, depth)
    pair_meta = pair(after(own_meta, query_own))

    def swap(sent):
        return jnp.stack([hop(one, "expert", k) if k else one for k, one in zip(mine, sent)])

    by_block = swap([jnp.stack([own_meta, pair_meta])] * len(mine)).reshape(devices, 18, depth)
    gain_one, gain_two = by_block[:, :1].astype(F32), by_block[:, 1:2].astype(F32)
    route_one, route_two = by_block[:, 2 : 2 + EA], by_block[:, 2 + EA :]

    belt = []

    def on_belt(values):
        belt.append(pair(after(values, belt[-2]) if len(belt) > 1 else values))
        return belt[-1]

    query_pair = [on_belt(query_own[at : at + 2]) for at in range(0, EA, 2)]
    query_ws = [[query_own], query_pair]

    blocks, scale_one, chunks = pack(
        places, after(tokens, query_own), routes_att, parts, devices
    )
    chunks[1] = after(chunks[1], by_block)
    came = after(swap(chunks), belt[0])
    token_pieces = gather_pieces(came, "tensor")
    dense_pieces = gather_pieces(
        after(jnp.concatenate([w_key, w_value], axis=1), came), "expert", far
    )
    normed_own, normed_pair, routes_far = unpack(
        [after(token_pieces[r], belt[2]) if r == 3 else token_pieces[r] for r in range(parts)],
        by_block[:2, 0].astype(F32),
    )
    normed_far = [normed_own, normed_pair]
    for k in mine:
        dense_pieces[k ^ 1] = on_belt(dense_pieces[k])
    dense_pieces = [dense_pieces[j] for j in range(devices)]
    normed_blocks = (blocks.astype(F32) * scale_one * gain_one).astype(BF16)
    output_own = after(w_output, normed_own).transpose(1, 0, 2)
    output_pair = [on_belt(output_own[at : at + 2]) for at in range(0, EA, 2)]
    output_ws = [[output_own], output_pair]
    routes_one = by_part(after(routes_att, normed_own))

    chosen_one = chosen_of(routes_one, EA)
    gates_one = pair_gates(
        jnp.einsum("jtd,jkd->tk", normed_blocks, route_one, preferred_element_type=F32), chosen_one
    )

    def project_sum(xs, ws):
        early = [k for k in mine if k & 2][::-1]
        middle = [k for k in mine if k and not k & 2]
        found = project(tuple(early), xs, ws, routes_far, BF16)
        chunks = [dict(zip(early, found[choice::2])) for choice in range(2)]
        came = [{k: hop(chunks[c][k], "expert", 2) for k in early} for c in range(2)]
        ready = after(xs[0], came[0][early[0]])
        found = project(tuple(middle), [ready, xs[1]], ws, routes_far, F32)
        sent = []
        for c in range(2):
            held = dict(zip(middle, found[c::2]))
            held = {k: (held[k] + came[c][k + 2].astype(F32)).astype(BF16) for k in middle}
            here = []
            for bit in far[:-1][::-1]:
                for k in sorted(held, reverse=True):
                    if k & bit:
                        sent.append(held.pop(k))
                        arrived = hop(sent[-1], "expert", bit)
                        if k == bit:
                            here.append(arrived)
                        else:
                            held[k ^ bit] = (held[k ^ bit].astype(F32) + arrived.astype(F32)).astype(BF16)
            came[c] = [came[c][2], *here]
        ready = after(xs[0], *sent)
        sums = list(project((0,), [ready, xs[1]], ws, routes_far, F32))
        for c in range(2):
            for one in came[c]:
                sums[c] = sums[c] + one.astype(F32)
        return sums, sent

    raw, started = project_sum(normed_far, query_ws)
    dense_raw = dense_rows(normed_blocks, dense_pieces)
    at_row = (order[:, None] * share + jnp.arange(share)).reshape(-1).astype(jnp.int32)
    at_row = after(at_row, *started)
    segment = by_part(after(segment_ids, *started)[0])
    tables = (*angles(at_row), segment[:, None], segment[None, :], at_row[:, None], at_row[None, :])

    routes_mlp = after(routes_mlp, *started)
    chosen_two = chosen_of(routes_mlp, EXPERTS)
    slot_part, slot = slots_of(chosen_two, quarter)
    slot = by_part(jnp.where(slot_part == part, slot, -1)).T
    routes_two = by_part(routes_mlp).T
    own_chosen = routes_two[:, None, :share] == jnp.arange(EXPERTS, dtype=jnp.int32)[None, :, None]
    own_chosen = own_chosen.astype(F32)
    up = arrange(places, after(cotangent, *started), parts, devices)
    own_up = up[:, :share].astype(F32)
    slots = EXPERTS * quarter

    raw = after(raw, slot, routes_two, own_chosen, up, *tables)
    query, key, lse, mixed, *mixed_sent = attend(raw, dense_raw, gates_one, tables)
    mixed_pieces = gather_far(*mixed_sent)
    branch = to_owners(mixed_pieces, routes_far, output_ws, parts)
    own_tokens = blocks[:, :share]
    hidden, scale_two, own_two = hidden_rows(own_tokens, gain_two, branch)

    rows, dexpert, gates_two = dispatch(
        places, slot, routes_two, route_two, up, gather_pieces(own_two, "tensor"), slots
    )

    def to_experts(values):
        shaped = values.reshape(EXPERTS, 1, quarter, D)
        shaped = jnp.broadcast_to(shaped, (EXPERTS, group, quarter, D)).reshape(devices, quarter, D)
        return lax.all_to_all(shaped, "expert", 0, 0, tiled=True).reshape(devices * quarter, D)

    def back_home(summed):
        summed = summed.astype(BF16).reshape(devices, quarter, D)
        back = lax.all_to_all(summed, "expert", 0, 0, tiled=True)
        back = back.reshape(EXPERTS, group, quarter, D)
        if group > 1:
            back = jnp.sum(back.astype(F32), axis=1).astype(BF16)
        return back.reshape(slots, D)

    turned = (((1,), (1,)), ((), ()))

    def forward(half):
        gate_pre = jnp.dot(half, w_gate[0], preferred_element_type=F32)
        up_pre = jnp.dot(half, w_up[0], preferred_element_type=F32)
        return gate_pre, up_pre, (jax.nn.silu(gate_pre) * up_pre).astype(BF16)

    def backward(half, gate_pre, up_pre):
        dacted = lax.dot_general(half, w_down[0], turned, preferred_element_type=F32)
        sigma = jax.nn.sigmoid(gate_pre)
        dup = (dacted * gate_pre * sigma).astype(BF16)
        dgate = (dacted * up_pre * sigma * (1.0 + gate_pre * (1.0 - sigma))).astype(BF16)
        dinput = lax.dot_general(dgate, w_gate[0], turned, preferred_element_type=F32)
        dinput += lax.dot_general(dup, w_up[0], turned, preferred_element_type=F32)
        return dgate, dup, dinput.astype(BF16)

    assert parts == 4
    came_rows = to_experts(rows)
    far_rows = hop(came_rows, "tensor", 2)
    row_halves = [jnp.concatenate([came_rows, hop(came_rows, "tensor", 1)])]
    pre = [forward(row_halves[0])]
    came_grads = to_experts(after(dexpert, came_rows))
    far_grads = hop(came_grads, "tensor", 2)
    far_rows = after(far_rows, came_grads, pre[0][2])
    row_halves.append(jnp.concatenate([far_rows, hop(far_rows, "tensor", 1)]))
    pre.append(forward(row_halves[1]))
    expert_part = [
        jnp.dot(acted, w_down[0], preferred_element_type=F32).astype(BF16)
        for _, _, acted in pre[::-1]
    ][::-1]

    pair_normed = pair(after(normed_far[1], came_grads))
    pair_routes = pair(after(routes_far, came_grads).astype(BF16).transpose(0, 2, 1))
    far_grads = after(far_grads, *expert_part, pair_normed, pair_routes)
    pair_routes = pair_routes.transpose(0, 2, 1).astype(jnp.int32)
    grad_halves = [
        jnp.concatenate([one, hop(one, "tensor", 1)]) for one in (came_grads, far_grads)
    ]

    def sum_far(half):
        far_chunk, last = jnp.split(half, 2)
        return (far_chunk.astype(F32) + hop(last, "tensor", 1).astype(F32)).astype(BF16)

    def sum_near(half, came):
        chunk, last = jnp.split(half, 2)
        return chunk.astype(F32) + hop(last, "tensor", 1).astype(F32) + came.astype(F32)

    expert_far = sum_far(expert_part[1])
    expert_out = back_home(sum_near(expert_part[0], hop(expert_far, "tensor", 2)))
    back_far = backward(
        after(grad_halves[1], *expert_part), *pre[1][:2]
    )
    input_far = sum_far(back_far[2])
    back_near = backward(
        after(grad_halves[0], input_far), *pre[0][:2]
    )
    input_near = sum_near(back_near[2], hop(input_far, "tensor", 2))
    dreturned = back_home(input_near)

    expert_rows, dout_rows = jnp.concatenate(row_halves), jnp.concatenate(grad_halves)
    acted = jnp.concatenate([one[2] for one in pre])
    dgate = jnp.concatenate([back_near[0], back_far[0]])
    dup = jnp.concatenate([back_near[1], back_far[1]])
    dgate, dup = after((dgate, dup), expert_out)
    grad_gate = jnp.einsum("rd,rf->df", expert_rows, dgate, preferred_element_type=F32)[None]

    *out_chunks, weighted = combine(places, slot, expert_out, parts, devices, gates_two, dexpert)
    weighted, _ = scatter_sum(
        {r: weighted[:, r * share : (r + 1) * share] for r in range(parts)}, "tensor"
    )
    grad_up = jnp.einsum("rd,rf->df", expert_rows, dup, preferred_element_type=F32)[None]
    dreturned = after(dreturned, grad_gate, grad_up)
    back_chunks = combine(places, slot, dreturned, parts, devices)
    own_gates_two = gates_two[:, :share]
    inner = weighted - own_gates_two * jnp.sum(weighted, axis=0, keepdims=True)
    own_dlogits = jnp.sum(inner[:, None, :] * own_chosen, axis=0)
    dnormed = scatter_sum(dict(enumerate(back_chunks)), "tensor")[0] + jnp.einsum(
        "kt,jkd->jtd", own_dlogits, route_two.astype(F32), precision=PRECISE
    )
    pulled = dnormed * gain_two
    inner_mean = jnp.sum(pulled * hidden, axis=(0, 2), keepdims=True) / D
    dhidden = own_up + scale_two * pulled - hidden * (scale_two * scale_two * scale_two * inner_mean)

    moe, _ = scatter_sum(dict(enumerate(after(out_chunks, dhidden))), "tensor")

    sent = dhidden.astype(BF16)
    up_pieces = gather_pieces(swap(
        [jnp.concatenate([sent[k], sent[k ^ 1]], axis=1) for k in mine]
    ), "tensor")
    dhidden_far = assemble([up_pieces[r] for r in range(parts)])
    pull, started = project_sum(dhidden_far, output_ws)
    grad_output, pair_grad = map_grads(
        [[after(dhidden_far[0], *started), dhidden_far[1]]],
        [routes_far],
        [half for k in mine for half in mixed_pieces[k]],
        (F32, BF16),
    )
    pair_grad = pair(pair_grad)
    mixed_out = output_rows(
        places, gather_pieces(after((hidden + moe).astype(BF16), *started), "tensor"), BF16
    )
    def to_features(partial):
        count = partial.shape[0]
        chunks = jnp.take(partial.transpose(1, 0, 2), me ^ jnp.arange(devices), axis=0)[:, None]
        chunks = jnp.broadcast_to(chunks, (devices, parts, count, depth)).reshape(-1, count, depth)
        return jnp.sum(lax.all_to_all(chunks, ("expert", "tensor"), 0, 0, tiled=True), axis=0)

    part_gain_two = jnp.sum(dnormed * hidden * scale_two, axis=1)[None]
    part_route_two = jnp.einsum(
        "kt,jtd->kjd", own_dlogits, own_two.astype(F32), precision=PRECISE
    )

    pull = after(pull, grad_output)
    *dqueries, ddense, dgates_one = attend_back(query, key, lse, mixed, pull, gates_one, tables)
    dquery_pieces = gather_far(*dqueries)
    acted = after(acted, dquery_pieces[2][0])
    grad_down = jnp.einsum("rf,rd->fd", acted, dout_rows, preferred_element_type=F32)[None]
    pair_dquery = {k: [pair(one) for one in dquery_pieces[k]] for k in mine}
    dense_far = gather_pieces(ddense, "expert", far)
    dense_back = dense_rows_back(ddense, dense_pieces, parts)
    dense_share, _ = scatter_sum({r: dense_back[r] for r in range(parts)}, "tensor")
    dnormed_came = to_owners(
        dquery_pieces,
        routes_far,
        query_ws,
        parts,
        ((*pair_dquery[0], grad_down), pair_dquery[2], pair_dquery[4]),
    )
    dgates_one, _ = scatter_sum(
        {r: dgates_one[r * share : (r + 1) * share] for r in range(parts)}, "tensor"
    )
    grad_dense, pair_grad_dense = dense_grad(
        normed_far, [dense_far[k] for k in mine], (F32, BF16)
    )
    grad_dense = grad_dense + pair(pair_grad_dense).astype(F32)
    (grad_query,) = map_grads(
        [[normed_far[0]], [after(pair_normed, *dnormed_came.values())]],
        [routes_far, pair_routes],
        [half for side in (dquery_pieces, pair_dquery) for k in mine for half in side[k]],
        (F32,),
    )
    grad_key, grad_value = grad_dense[:, :width], grad_dense[:, width:]

    own_gates, own_scale = gates_one[:share], scale_one[:share]
    own_dlogits_one = logit_grad(own_gates, own_gates * dgates_one, chosen_one[:share])
    dnormed_came[0] = after(dnormed_came[0], *pair_dquery[6], dense_far[4])
    whole = jnp.stack(
        [
            dnormed_came[k][:, b * depth : (b + 1) * depth].astype(F32)
            for k in mine
            for b in range(2)
        ]
    )
    dnormed_one = whole + dense_share + jnp.einsum(
        "tk,jkd->jtd", own_dlogits_one, route_one.astype(F32), precision=PRECISE
    )
    pulled_one = dnormed_one * gain_one
    token_rows = own_tokens.astype(F32)
    inner_one = jnp.sum(pulled_one * token_rows, axis=(0, 2), keepdims=True) / D
    own_grad = (
        dhidden
        + own_scale * pulled_one
        - token_rows * (own_scale * own_scale * own_scale * inner_one)
    )
    own_grad = after(own_grad.astype(BF16), dense_far[6])
    grad_pieces = gather_pieces(own_grad, "tensor")
    grad_tokens = output_rows(places, {**grad_pieces, 3: after(grad_pieces[3], grad_dense)}, F32)
    part_gain_one = jnp.sum(dnormed_one * token_rows * own_scale, axis=1)[None]
    part_route_one = jnp.einsum(
        "tk,jtd->kjd", own_dlogits_one, normed_blocks[:, :share].astype(F32), precision=PRECISE
    )

    smalls = to_features(
        jnp.concatenate([part_gain_two, part_route_two, part_gain_one, part_route_one])
    )
    small_two, small_one = smalls[:9], smalls[9:]
    return (
        mixed_out,
        grad_tokens,
        small_one[0],
        small_one[1:].T,
        grad_query,
        grad_key,
        grad_value,
        grad_output + pair_grad.astype(F32),
        small_two[0],
        small_two[1:].T,
        grad_gate,
        grad_up,
        grad_down,
    )


def solution(mesh):
    in_specs = (
        P("expert", None),
        P("expert", None),
        P("expert", None),
        P("expert", None),
        P("expert", None),
        P("expert"),
        P("expert", None),
        P("expert", None, "tensor"),
        P("expert", "tensor"),
        P("expert", "tensor"),
        P("expert", None, "tensor"),
        P("expert"),
        P("expert", None),
        P("expert", None, "tensor"),
        P("expert", None, "tensor"),
        P("expert", "tensor", None),
    )
    out_specs = (
        P("expert", None),
        P("expert", None),
        P("expert"),
        P("expert", None),
        P("expert", None, "tensor"),
        P("expert", "tensor"),
        P("expert", "tensor"),
        P("expert", None, "tensor"),
        P("expert"),
        P("expert", None),
        P("expert", None, "tensor"),
        P("expert", None, "tensor"),
        P("expert", "tensor", None),
    )
    return jax.shard_map(body, mesh=mesh, in_specs=in_specs, out_specs=out_specs, check_vma=False)
```
